32 devices in a mesh: wide: 8 (over z, y), tm: 4 (over x, core).
Axes of the slice: x: 2, y: 2, z: 4, core: 2. Of those that a mesh axis runs over, the one named last changes fastest.
Arguments:
- voltages: bfloat16 [2, 2048, 24576], P(None, 'wide', 'tm'), may hold values from -12 to 12
- fir_taps: float32 [4, 256], replicated, may hold values from -3 to 3
- steering: float32 [512, 2048], replicated, may hold values from 0 to 8
- band_widths: int32 [8], replicated, may hold values from 1 to 64, 256 in all
- delays: int32 [128, 256], replicated, may hold values from 0 to 7, as said below
- box_widths: int32 [4], replicated, may hold values from 1 to 8, as said below
Outputs:
- significance: float32 [128, 4, 96, 512], P(None, None, 'tm', 'wide')
The draws below stay inside these ranges and needn't reach their ends.
Inputs may be any that keep to these rules, and one draw needn't show every extreme that they name: `band_widths`: the widths sum to 256; some band has exactly 64 channels. `delays`: the value 7 occurs in every draw. `box_widths`: the value 8 occurs in every draw.
All inputs are finite; a program needn't handle non-finite values.
Results may differ from the reference program's by a relative error of at most 0.0003.
The reference program's roundings to bfloat16 on the way count: a program that leaves them out, or rounds other values in their place, can miss the bound.
Values may be sent and summed in bfloat16 or wider, within the bound.
No kernel may reach another device: no remote copies, remote signals or barrier semaphores. Data moves between devices by JAX's collectives and lax.ppermute only.
A program may use at most 128 MiB of HBM per device.

```python
import math
import jax
import jax.numpy as jnp
import numpy as np
from jax import lax

ANTENNA_COUNT = 2048
CHANS = 256
BEAM_TOTAL = 512
TRIALS = 128
TAPS = 4
MAXDELAY = 7
WMAX = 8
NWID = 4
FRAMES = 96
VOLTAGE_SAMPLES = 24576
BANDS = 8
MOST_BAND = 64


def draw_voltages(key, part):
    primary_key = jax.random.fold_in(key, 0)
    ramp = jnp.arange(VOLTAGE_SAMPLES, dtype=jnp.float32) / VOLTAGE_SAMPLES
    envelope = jnp.sqrt(1.0 + 4.0 * ramp)
    value_rows = jnp.clip(jax.random.normal(primary_key, (2, ANTENNA_COUNT, VOLTAGE_SAMPLES), jnp.float32), -5.0, 5.0)
    value_rows = value_rows * envelope
    return value_rows.astype(jnp.bfloat16)


def draw_delays(key, part):
    primary_key, key_marked = jax.random.split(key)
    value_rows = jax.random.randint(primary_key, (TRIALS, CHANS), 0, MAXDELAY + 1, jnp.int32)
    marked = jax.random.randint(key_marked, (), 0, TRIALS * CHANS, jnp.int32)
    flat_index = jnp.arange(TRIALS * CHANS, dtype=jnp.int32).reshape(TRIALS, CHANS)
    return jnp.where(flat_index == marked, MAXDELAY, value_rows).astype(jnp.int32)


def draw_box_widths(key, part):
    primary_key, key_marked = jax.random.split(key)
    value_rows = jax.random.randint(primary_key, (NWID,), 1, WMAX + 1, jnp.int32)
    marked = jax.random.randint(key_marked, (), 0, NWID, jnp.int32)
    return jnp.where(jnp.arange(NWID, dtype=jnp.int32) == marked, WMAX, value_rows).astype(jnp.int32)


def length_profile(count, total, most, skew):
    weights = [(1 << 20) // math.isqrt(rank ** skew) + 1 for rank in range(2, count + 1)]
    rest, given = total - most - (count - 1), [1] * (count - 1)
    while rest > 0:
        movable = [i for i in range(count - 1) if given[i] < most]
        pool, budget = sum([weights[i] for i in movable]), rest
        for i in movable:
            more = min(most - given[i], max(1, budget * weights[i] // pool), rest)
            given[i] = given[i] + more
            rest = rest - more
    return np.array([most] + given)


def uneven(rng, count, total, most, slope):
    if count == 2:
        one = jax.random.randint(rng, (), max(1, total - most), min(most, total - 1) + 1)
        return jnp.stack([one, total - one])
    lengths = jnp.asarray(length_profile(count, total, most, slope), jnp.int32)
    pairs = (count - 1) // 2
    giver, taker = lengths[1:1 + 2 * pairs:2], lengths[2:2 + 2 * pairs:2]
    slack = jnp.minimum(giver - 1, most - taker)
    moved = jax.random.randint(jax.random.fold_in(rng, 1), (pairs,), 0, 1 << 20) % (slack + 1)
    lengths = lengths.at[1:1 + 2 * pairs:2].set(giver - moved).at[2:2 + 2 * pairs:2].set(taker + moved)
    return lengths[jax.random.permutation(jax.random.fold_in(rng, 2), count)]


def gaussian(rng, dims, width, reach, held_as=jnp.bfloat16):
    values = jax.random.normal(rng, dims, jnp.float32) * width
    return jnp.minimum(jnp.maximum(values, -reach), reach).astype(held_as)


def setup_inputs(seed: int = 0) -> dict:
    streams_of = jax.random.split(jax.random.key(seed), 7)
    voltages = draw_voltages(jax.random.fold_in(streams_of[6], 71), 0)
    fir_taps = gaussian(streams_of[1], (TAPS, CHANS), 0.5, 3.0, jnp.float32)
    steering = jnp.clip(jax.random.uniform(streams_of[2], (BEAM_TOTAL, ANTENNA_COUNT), jnp.float32, 0.0, 8.0), 0.0, 8.0)
    band_widths = uneven(streams_of[3], BANDS, CHANS, MOST_BAND, 1).astype(jnp.int32)
    delays = draw_delays(jax.random.fold_in(streams_of[6], 71), 0)
    box_widths = draw_box_widths(jax.random.fold_in(streams_of[6], 71), 0)
    return dict(voltages=voltages, fir_taps=fir_taps, steering=steering, band_widths=band_widths, delays=delays, box_widths=box_widths)


def dft_table(channel_rows):
    positions = jnp.arange(channel_rows, dtype=jnp.int32)
    product = positions[:, None] * positions[None, :] % channel_rows
    angles = 2.0 * math.pi / channel_rows * product.astype(jnp.float32)
    cosine = jnp.cos(angles)
    sines = jnp.sin(angles)
    upper_rows = jnp.concatenate([cosine, -sines], axis=1)
    lower_rows = jnp.concatenate([sines, cosine], axis=1)
    return jnp.stack([upper_rows, lower_rows]).astype(jnp.bfloat16)

def beam_weights(channel_ids, steering, channel_rows):
    frequency = 1.0 + channel_ids.astype(jnp.float32) / channel_rows
    phases = 2.0 * math.pi * (frequency[:, None, None] * steering[None, :, :])
    return jnp.concatenate([jnp.cos(phases), jnp.sin(phases)], axis=1).astype(jnp.bfloat16)

def beam_power(products, beam_count):
    real_in = products[:, :, 0, :]
    imag_in = products[:, :, 1, :]
    beam_real = real_in[..., :beam_count] + imag_in[..., beam_count:]
    beam_imag = imag_in[..., :beam_count] - real_in[..., beam_count:]
    return beam_real * beam_real + beam_imag * beam_imag

def reference(voltages, fir_taps, steering, band_widths, delays, box_widths):
    channel_rows = CHANS
    frame_rows = FRAMES
    block_length = math.gcd(ANTENNA_COUNT, 64)
    input_signal = voltages.reshape(2, ANTENNA_COUNT // block_length, block_length, frame_rows, channel_rows)
    input_signal = jnp.moveaxis(input_signal, 1, 0)
    table = dft_table(channel_rows).astype(jnp.float32)

    def spectrum_block(piece):
        filter_output = jnp.zeros((2, block_length, frame_rows, channel_rows), jnp.float32)
        for tap_index in range(TAPS):
            filter_output = filter_output + fir_taps[tap_index] * jnp.roll(piece, tap_index, axis=2).astype(jnp.float32)
        filter_output = filter_output.astype(jnp.bfloat16).astype(jnp.float32)
        return jnp.einsum('pafn,pnq->afq', filter_output, table).astype(jnp.bfloat16)
    spectrum_rows = lax.map(spectrum_block, input_signal).reshape(ANTENNA_COUNT, frame_rows, 2, channel_rows)
    by_channel = jnp.moveaxis(spectrum_rows, 3, 0)

    def form_channel(channel_index):
        gathered = jnp.take(by_channel, channel_index[None], axis=0)
        gathered = jnp.moveaxis(gathered, 0, 3).astype(jnp.float32)
        weights = beam_weights(channel_index[None], steering, channel_rows).astype(jnp.float32)
        products = jnp.einsum('afpm,mya->mfpy', gathered, weights)
        return beam_power(products, BEAM_TOTAL)[0]
    powers = lax.map(form_channel, jnp.arange(channel_rows, dtype=jnp.int32))
    starts = jnp.cumsum(band_widths) - band_widths
    channel_ids = jnp.arange(channel_rows, dtype=jnp.int32)
    channel_band = lax.optimization_barrier(jnp.sum((channel_ids[:, None] >= starts[None, :]).astype(jnp.int32), axis=1)) - 1
    band_onehot = (channel_band[:, None] == jnp.arange(BANDS, dtype=jnp.int32)[None, :]).astype(jnp.float32)
    channel_sums = lax.optimization_barrier(jnp.sum(powers, axis=(1, 2)))
    band_total = lax.optimization_barrier(jnp.sum(channel_sums[:, None] * band_onehot, axis=0))
    band_mean = band_total / (band_widths.astype(jnp.float32) * (frame_rows * BEAM_TOTAL))
    channel_mean = lax.optimization_barrier(jnp.sum(band_onehot * band_mean[None, :], axis=1))
    levels = (powers / channel_mean[:, None, None]).astype(jnp.bfloat16)
    dedispersed = jnp.zeros((TRIALS, frame_rows * BEAM_TOTAL), jnp.float32)
    for delay_step in range(MAXDELAY + 1):
        rolled = jnp.roll(levels, -delay_step, axis=1).reshape(channel_rows, frame_rows * BEAM_TOTAL)
        selector = (delays == delay_step).astype(jnp.bfloat16)
        dedispersed = dedispersed + jnp.dot(selector, rolled, preferred_element_type=jnp.float32)
    dedispersed = dedispersed.reshape(TRIALS, frame_rows, BEAM_TOTAL)
    window = jnp.zeros((TRIALS, NWID, frame_rows, BEAM_TOTAL), jnp.float32)
    for lag_frames in range(WMAX):
        inside = (box_widths > lag_frames).astype(jnp.float32)
        window = window + inside[None, :, None, None] * jnp.roll(dedispersed, -lag_frames, axis=1)[:, None, :, :]
    expected = box_widths.astype(jnp.float32) * channel_rows
    return (window - expected[None, :, None, None]) / jnp.sqrt(expected)[None, :, None, None]
```

```python
import functools
import math

import jax
import jax.numpy as jnp
import numpy as np
from jax import lax
from jax.experimental import pallas as pl
from jax.experimental.pallas import tpu as pltpu
from jax.sharding import PartitionSpec as P

MAXDELAY = 7
WMAX = 8
AXES = ("wide", "tm")
MIB = 1 << 20


def dft_rows(channel_rows):
    positions = np.arange(channel_rows, dtype=np.int64)
    product = (positions[:, None] * positions[None, :] % channel_rows).astype(np.float32)
    angles = np.float32(2.0 * math.pi / channel_rows) * product
    cosine = np.cos(angles.astype(np.float64)).astype(np.float32)
    sines = np.sin(angles.astype(np.float64)).astype(np.float32)
    real_rows = np.concatenate([cosine.T, sines.T], axis=1)
    imag_rows = np.concatenate([-sines.T, cosine.T], axis=1)
    rows = np.stack([real_rows, imag_rows], axis=1).reshape(2 * channel_rows, 2 * channel_rows)
    return rows.astype(jnp.bfloat16)


def spectra_kernel(taps_ref, table_ref, halo_ref, volt_ref, out_ref, ring_ref, part_ref):
    taps = taps_ref.shape[0]
    width = taps_ref.shape[1]
    frame = pl.program_id(0) * 8 + pl.program_id(1)
    inner = pl.program_id(1)

    @pl.when(frame == 0)
    def _():
        for back in range(1, taps):
            ring_ref[(taps - back) % taps] = halo_ref[
                :, :, (taps - 1 - back) * width : (taps - back) * width
            ]

    ring_ref[frame % taps] = volt_ref[...]
    pieces = []
    for part in range(2):
        total = None
        for back in range(taps):
            value = ring_ref[(frame + taps - back) % taps, part].astype(jnp.float32)
            term = taps_ref[back : back + 1, :] * value
            total = term if total is None else total + term
        pieces.append(total.astype(jnp.bfloat16))
    filtered = jnp.concatenate(pieces, axis=1)
    spectrum = lax.dot_general(
        table_ref[...], filtered, (((1,), (1,)), ((), ())), preferred_element_type=jnp.float32
    )
    rows, antennas = spectrum.shape
    lanes = part_ref.shape[0] * 128
    if lanes > antennas:
        spectrum = jnp.concatenate(
            [spectrum, jnp.zeros((rows, lanes - antennas), jnp.float32)], axis=1
        )
    for half in range(lanes // 128):
        part_ref[half, pl.ds(inner, rows, stride=8), :] = spectrum[:, half * 128 : half * 128 + 128]

    @pl.when(inner == 7)
    def _():
        for half in range(lanes // 128):
            size = min(128, antennas - half * 128)
            value = part_ref[half].astype(jnp.bfloat16).reshape(rows // 2, 16, 128)
            out_ref[:, 0, :, half * 128 : half * 128 + size] = value[:, :, :size]


def spectra(voltages, halo, fir_taps):
    taps, width = fir_taps.shape
    antennas = voltages.shape[1]
    frames = voltages.shape[2] // width
    groups = frames // 8
    table = jnp.asarray(dft_rows(width))
    return pl.pallas_call(
        spectra_kernel,
        grid=(groups, 8),
        in_specs=[
            pl.BlockSpec(fir_taps.shape, lambda g, i: (0, 0)),
            pl.BlockSpec(table.shape, lambda g, i: (0, 0)),
            pl.BlockSpec(halo.shape, lambda g, i: (0, 0, 0)),
            pl.BlockSpec((2, antennas, width), lambda g, i: (0, 0, g * 8 + i)),
        ],
        out_specs=pl.BlockSpec((width, 1, 16, antennas), lambda g, i: (0, g, 0, 0)),
        out_shape=jax.ShapeDtypeStruct((width, groups, 16, antennas), jnp.bfloat16),
        scratch_shapes=[
            pltpu.VMEM((taps, 2, antennas, width), jnp.bfloat16),
            pltpu.VMEM((-(-antennas // 128), 2 * width * 8, 128), jnp.float32),
        ],
        compiler_params=pltpu.CompilerParams(vmem_limit_bytes=48 * MIB),
        cost_estimate=pl.CostEstimate(
            flops=2 * frames * antennas * 4 * width * width,
            bytes_accessed=8 * frames * antennas * width,
            transcendentals=0,
        ),
        name="spectra",
    )(fir_taps, table, halo, voltages)


def sincos(phase):
    turns = jnp.round(phase * np.float32(1.0 / (2.0 * math.pi)))
    high = np.float32(6.28125)
    middle = np.float32(np.round((2.0 * math.pi - 6.28125) * 2.0**26) / 2.0**26)
    low = np.float32(2.0 * math.pi - 6.28125 - float(middle))
    rest = phase - turns * high
    rest = rest - turns * middle
    rest = rest - turns * low
    square = rest * rest
    s = np.float32(SIN_COEF[-1])
    for value in SIN_COEF[-2::-1]:
        s = s * square + np.float32(value)
    s = s * rest
    c = np.float32(COS_COEF[-1])
    for value in COS_COEF[-2::-1]:
        c = c * square + np.float32(value)
    return np.float32(1.0) - s * s, s * c


def half_angle_coefficients():
    top = (math.pi + 0.01) ** 2
    nodes = (np.cos((np.arange(400) + 0.5) * math.pi / 400) + 1.0) * 0.5 * top
    root = np.sqrt(nodes)
    fits = []
    for values, order in (
        (math.sqrt(2.0) * np.sin(root / 2) / root, 5),
        (math.sqrt(2.0) * np.cos(root / 2), 6),
    ):
        fit = np.polynomial.chebyshev.Chebyshev.fit(nodes, values, order - 1, domain=[0.0, top])
        fits.append([float(v) for v in fit.convert(kind=np.polynomial.Polynomial).coef])
    return fits


SIN_COEF, COS_COEF = half_angle_coefficients()


def weights_kernel(freq_ref, steer_ref, out_ref):
    channel = pl.program_id(1)
    beams = steer_ref.shape[1]
    frequency = freq_ref[channel]
    rows = steer_ref.shape[0]

    def step(index, carry):
        at = pl.ds(pl.multiple_of(index * 16, 16), 16)
        phase = np.float32(2.0 * math.pi) * (frequency * steer_ref[at, :])
        cosine, sines = sincos(phase)
        out_ref[0, at, :beams] = cosine.astype(jnp.bfloat16)
        out_ref[0, at, beams:] = sines.astype(jnp.bfloat16)
        return carry

    lax.fori_loop(0, rows // 16, step, 0)


def beam_weights(frequency, steering_t):
    antennas, beams = steering_t.shape
    channels = frequency.shape[0]
    block = min(512, antennas)
    return pl.pallas_call(
        weights_kernel,
        grid=(antennas // block, channels),
        in_specs=[
            pl.BlockSpec(memory_space=pltpu.SMEM),
            pl.BlockSpec((block, beams), lambda a, c: (a, 0)),
        ],
        out_specs=pl.BlockSpec((1, block, 2 * beams), lambda a, c: (c, a, 0)),
        out_shape=jax.ShapeDtypeStruct((channels, antennas, 2 * beams), jnp.bfloat16),
        compiler_params=pltpu.CompilerParams(vmem_limit_bytes=32 * MIB),
        cost_estimate=pl.CostEstimate(
            flops=30 * channels * antennas * beams,
            bytes_accessed=4 * channels * antennas * beams,
            transcendentals=2 * channels * antennas * beams,
        ),
        name="weights",
    )(frequency, steering_t)


def beam_kernel(wide, tm, data_ref, weight_ref, power_ref, sum_ref, gather_ref, acc_ref):
    channel = pl.program_id(0)
    groups = data_ref.shape[2]
    antennas = data_ref.shape[4]
    rows = groups * 16
    for w in range(wide):
        for m in range(tm):
            gather_ref[m * rows : (m + 1) * rows, w * antennas : (w + 1) * antennas] = data_ref[
                w * tm + m, 0
            ].reshape(rows, antennas)
    products = jnp.dot(gather_ref[...], weight_ref[0], preferred_element_type=jnp.float32)
    beams = products.shape[1] // 2
    products = products.reshape(tm * groups, 2, 8, 2 * beams)
    real_in = products[:, 0]
    imag_in = products[:, 1]
    beam_real = real_in[..., :beams] + imag_in[..., beams:]
    beam_imag = imag_in[..., :beams] - real_in[..., beams:]
    power = beam_real * beam_real + beam_imag * beam_imag
    power_ref[0] = power.reshape(tm * groups * 8, beams)
    total = jnp.sum(jnp.sum(power, axis=0), axis=(0, 1), keepdims=True)
    lane = lax.broadcasted_iota(jnp.int32, acc_ref.shape, 1)

    @pl.when(channel == 0)
    def _():
        acc_ref[...] = jnp.zeros_like(acc_ref)

    acc_ref[...] = jnp.where(lane == channel, total, acc_ref[...])

    @pl.when(channel == pl.num_programs(0) - 1)
    def _():
        sum_ref[...] = jnp.broadcast_to(acc_ref[...], sum_ref.shape)


def form_beams(received, weights, wide, tm):
    devices, channels, groups, _, antennas = received.shape
    _, antenna_full, twice = weights.shape
    frames = tm * groups * 8
    beams = twice // 2
    return pl.pallas_call(
        functools.partial(beam_kernel, wide, tm),
        grid=(channels,),
        in_specs=[
            pl.BlockSpec((devices, 1, groups, 16, antennas), lambda c: (0, c, 0, 0, 0)),
            pl.BlockSpec((1, antenna_full, twice), lambda c: (c, 0, 0)),
        ],
        out_specs=[
            pl.BlockSpec((1, frames, beams), lambda c: (c, 0, 0)),
            pl.BlockSpec((devices, 128), lambda c: (0, 0)),
        ],
        out_shape=[
            jax.ShapeDtypeStruct((channels, frames, beams), jnp.float32),
            jax.ShapeDtypeStruct((devices, 128), jnp.float32),
        ],
        scratch_shapes=[
            pltpu.VMEM((2 * frames, antenna_full), jnp.bfloat16),
            pltpu.VMEM((1, 128), jnp.float32),
        ],
        compiler_params=pltpu.CompilerParams(vmem_limit_bytes=48 * MIB),
        cost_estimate=pl.CostEstimate(
            flops=4 * channels * frames * antenna_full * twice,
            bytes_accessed=2 * channels * antenna_full * twice,
            transcendentals=0,
        ),
        name="beams",
    )(received, weights)


def level_kernel(wide, tm, reach, mask_ref, count_ref, sums_ref, power_ref, out_ref):
    channels, frames, beams = power_ref.shape
    own_beams = beams // wide
    own_frames = frames // tm
    per_row = max(1, 128 // own_beams)
    sums = sums_ref[...]
    means = []
    for c in range(channels):
        means.append(jnp.sum(jnp.sum(mask_ref[c] * sums, axis=0, keepdims=True), axis=1, keepdims=True))
    mean = jnp.concatenate(means, axis=0) / count_ref[...]
    span = own_frames + reach

    def level(f):
        value = jnp.concatenate([power_ref[c, f : f + 1, :] for c in range(channels)], axis=0)
        return (value / mean).astype(jnp.bfloat16)

    for start in range(0, frames, per_row):
        values = [level(f) for f in range(start, start + per_row)]
        for w in range(wide):
            piece = jnp.concatenate(
                [v[:, w * own_beams : (w + 1) * own_beams] for v in values], axis=1
            )
            for m in range(tm):
                for lap in (0, frames):
                    at = start + lap - m * own_frames
                    if 0 <= at < span:
                        width = min(per_row, span - at) * own_beams
                        out_ref[w * tm + m, :, at * own_beams : at * own_beams + width] = piece[
                            :, :width
                        ]


def form_levels(mask, count, sums, powers, wide, tm, reach):
    channels, frames, beams = powers.shape
    span = frames // tm + reach
    lanes = span * (beams // wide)
    return pl.pallas_call(
        functools.partial(level_kernel, wide, tm, reach),
        out_shape=jax.ShapeDtypeStruct((wide * tm, channels, lanes), jnp.bfloat16),
        compiler_params=pltpu.CompilerParams(vmem_limit_bytes=48 * MIB),
        name="levels",
    )(mask, count, sums, powers)


def search_kernel(own_frames, width_ref, pick_ref, level_ref, out_ref, acc_ref):
    trials = pick_ref.shape[1]
    widths = out_ref.shape[1]
    beams = out_ref.shape[3]
    channels = pick_ref.shape[2]
    span = (own_frames + WMAX - 1) * beams
    for delay in range(MAXDELAY + 1):
        value = jnp.dot(
            pick_ref[delay],
            level_ref[:, delay * beams : delay * beams + span],
            preferred_element_type=jnp.float32,
        )
        if delay == 0:
            acc_ref[...] = value
        else:
            acc_ref[...] += value
    window = own_frames * beams
    shifts = [acc_ref[:, lag * beams : lag * beams + window] for lag in range(WMAX)]
    for i in range(widths):
        total = shifts[0]
        for lag in range(1, WMAX):
            inside = (width_ref[i] > lag).astype(jnp.float32)
            total = total + inside * shifts[lag]
        expected = width_ref[i].astype(jnp.float32) * np.float32(channels)
        root = jnp.sqrt(jnp.full((1, window), expected, jnp.float32))
        result = (total - expected) / root
        for f in range(own_frames):
            out_ref[:, i, f, :] = result[:, f * beams : (f + 1) * beams]


def search(box_widths, picks, levels, own_frames, own_beams):
    trials = picks.shape[1]
    widths = box_widths.shape[0]
    return pl.pallas_call(
        functools.partial(search_kernel, own_frames),
        in_specs=[
            pl.BlockSpec(memory_space=pltpu.SMEM),
            pl.BlockSpec(memory_space=pltpu.VMEM),
            pl.BlockSpec(memory_space=pltpu.VMEM),
        ],
        out_shape=jax.ShapeDtypeStruct((trials, widths, own_frames, own_beams), jnp.float32),
        scratch_shapes=[pltpu.VMEM((trials, (own_frames + WMAX - 1) * own_beams), jnp.float32)],
        compiler_params=pltpu.CompilerParams(vmem_limit_bytes=48 * MIB),
        name="search",
    )(box_widths, picks, levels)


def exchange(value):
    return lax.all_to_all(value, AXES, split_axis=0, concat_axis=0, tiled=True)


def body(voltages, fir_taps, steering, band_widths, delays, box_widths):
    wide = lax.axis_size("wide")
    tm = lax.axis_size("tm")
    devices = wide * tm
    taps, channel_rows = fir_taps.shape
    antenna_local = voltages.shape[1]
    beam_count = steering.shape[0]
    sample_count = voltages.shape[2]
    frame_rows = sample_count // channel_rows
    total_frames = frame_rows * tm
    slots = channel_rows // devices
    own = lax.axis_index("wide") * tm + lax.axis_index("tm")
    own_ids = own * slots + jnp.arange(slots, dtype=jnp.int32)

    lookback = (taps - 1) * channel_rows
    halo = lax.ppermute(
        voltages[:, :, sample_count - lookback :], "tm", [(i, (i + 1) % tm) for i in range(tm)]
    )
    outgoing = spectra(voltages, halo, fir_taps)
    groups = frame_rows // 8
    received = exchange(outgoing.reshape(devices, slots * groups * 16, antenna_local))
    received = received.reshape(devices, slots, groups, 16, antenna_local)

    frequency = 1.0 + own_ids.astype(jnp.float32) / channel_rows
    weights = beam_weights(frequency, steering.T)
    powers, sums = form_beams(received, weights, wide, tm)

    starts = jnp.cumsum(band_widths) - band_widths
    ids = jnp.arange(channel_rows, dtype=jnp.int32)
    bands = jnp.sum((ids[:, None] >= starts[None, :]).astype(jnp.int32), axis=1) - 1
    own_band = jnp.sum((own_ids[:, None] >= starts[None, :]).astype(jnp.int32), axis=1) - 1
    mask = (own_band[:, None] == bands[None, :]).astype(jnp.float32)
    mask = jnp.pad(mask.reshape(slots, devices, slots), ((0, 0), (0, 0), (0, 128 - slots)))
    count = jnp.sum(
        jnp.where(
            own_band[:, None] == jnp.arange(band_widths.shape[0], dtype=jnp.int32)[None, :],
            band_widths.astype(jnp.float32)[None, :] * (total_frames * beam_count),
            0.0,
        ),
        axis=1,
        keepdims=True,
    )
    reach = MAXDELAY + WMAX - 1
    levels = form_levels(mask, count, exchange(sums), powers, wide, tm, reach)
    arrived = exchange(levels).reshape(channel_rows, levels.shape[2])

    steps = jnp.arange(MAXDELAY + 1, dtype=jnp.int32)
    picks = (delays[None, :, :] == steps[:, None, None]).astype(jnp.bfloat16)
    return search(box_widths, picks, arrived, frame_rows, beam_count // wide)


def solution(mesh):
    return jax.shard_map(
        body,
        mesh=mesh,
        in_specs=(P(None, "wide", "tm"), P(), P(), P(), P(), P()),
        out_specs=P(None, None, "tm", "wide"),
        check_vma=False,
    )
```

```python
import functools
import math

import jax
import jax.numpy as jnp
import numpy as np
from jax import lax
from jax.experimental import pallas as pl
from jax.experimental.pallas import tpu as pltpu
from jax.sharding import PartitionSpec as P

MAXDELAY = 7
WMAX = 8
AXES = ("wide", "tm")
MIB = 1 << 20


def dft_rows(channel_rows):
    positions = np.arange(channel_rows, dtype=np.int64)
    product = (positions[:, None] * positions[None, :] % channel_rows).astype(np.float32)
    angles = np.float32(2.0 * math.pi / channel_rows) * product
    cosine = np.cos(angles.astype(np.float64)).astype(np.float32)
    sines = np.sin(angles.astype(np.float64)).astype(np.float32)
    real_rows = np.concatenate([cosine.T, sines.T], axis=1)
    imag_rows = np.concatenate([-sines.T, cosine.T], axis=1)
    rows = np.stack([real_rows, imag_rows], axis=1).reshape(2 * channel_rows, 2 * channel_rows)
    return rows.astype(jnp.bfloat16)


def spectra_kernel(skip, taps_ref, table_ref, past_ref, volt_ref, *rest):
    out_ref, part_ref = rest[-2:]
    taps = taps_ref.shape[0]
    width = taps_ref.shape[1]
    for inner in range(8):
        pieces = []
        for part in range(2):
            total = None
            for back in range(taps):
                if inner >= back:
                    at = (inner - back) * width
                    value = volt_ref[part, :, at : at + width]
                else:
                    at = skip + (taps - 1 + inner - back) * width
                    value = past_ref[part, :, at : at + width]
                term = taps_ref[back : back + 1, :] * value.astype(jnp.float32)
                total = term if total is None else total + term
            pieces.append(total.astype(jnp.bfloat16))
        filtered = jnp.concatenate(pieces, axis=1)
        spectrum = lax.dot_general(
            table_ref[...], filtered, (((1,), (1,)), ((), ())), preferred_element_type=jnp.float32
        )
        rows, antennas = spectrum.shape
        lanes = part_ref.shape[0] * 128
        if lanes > antennas:
            spectrum = jnp.concatenate(
                [spectrum, jnp.zeros((rows, lanes - antennas), jnp.float32)], axis=1
            )
        for half in range(lanes // 128):
            part_ref[half, pl.ds(inner, rows, stride=8), :] = spectrum[
                :, half * 128 : half * 128 + 128
            ]
    for half in range(lanes // 128):
        size = min(128, antennas - half * 128)
        value = part_ref[half].astype(jnp.bfloat16).reshape(rows // 2, 16, 128)
        out_ref[:, 0, :, half * 128 : half * 128 + size] = value[:, :, :size]


def spectra(table, past, voltages, fir_taps, earlier=None):
    taps, width = fir_taps.shape
    antennas = voltages.shape[1]
    groups = voltages.shape[2] // (8 * width)
    first = 1 if earlier is None else 0
    steps = groups - 1 if earlier is None else 1
    operands = [fir_taps, table, past, voltages]
    in_specs = [
        pl.BlockSpec(fir_taps.shape, lambda g: (0, 0)),
        pl.BlockSpec(table.shape, lambda g: (0, 0)),
        pl.BlockSpec((2, antennas, 4 * width), lambda g: (0, 0, 2 * g + 1))
        if earlier is None
        else pl.BlockSpec(past.shape, lambda g: (0, 0, 0)),
        pl.BlockSpec((2, antennas, 8 * width), lambda g: (0, 0, g + first)),
    ]
    if earlier is not None:
        operands.append(earlier)
        in_specs.append(pl.BlockSpec(memory_space=pl.ANY))
    return pl.pallas_call(
        functools.partial(spectra_kernel, (5 - taps) * width if earlier is None else 0),
        grid=(steps,),
        in_specs=in_specs,
        out_specs=pl.BlockSpec((width, 1, 16, antennas), lambda g: (0, g + first, 0, 0)),
        out_shape=jax.ShapeDtypeStruct((width, groups, 16, antennas), jnp.bfloat16),
        scratch_shapes=[
            pltpu.VMEM((-(-antennas // 128), 2 * width * 8, 128), jnp.float32),
        ],
        input_output_aliases={} if earlier is None else {4: 0},
        compiler_params=pltpu.CompilerParams(vmem_limit_bytes=48 * MIB),
        cost_estimate=pl.CostEstimate(
            flops=64 * steps * antennas * width * width,
            bytes_accessed=64 * steps * antennas * width,
            transcendentals=0,
        ),
        name="spectra",
    )(*operands)


def sincos(phase):
    turns = jnp.round(phase * np.float32(1.0 / (2.0 * math.pi)))
    high = np.float32(6.28125)
    middle = np.float32(np.round((2.0 * math.pi - 6.28125) * 2.0**26) / 2.0**26)
    low = np.float32(2.0 * math.pi - 6.28125 - float(middle))
    rest = phase - turns * high
    rest = rest - turns * middle
    rest = rest - turns * low
    square = rest * rest
    s = np.float32(SIN_COEF[-1])
    for value in SIN_COEF[-2::-1]:
        s = s * square + np.float32(value)
    s = s * rest
    c = np.float32(COS_COEF[-1])
    for value in COS_COEF[-2::-1]:
        c = c * square + np.float32(value)
    return np.float32(1.0) - s * s, s * c


def half_angle_coefficients():
    top = (math.pi + 0.01) ** 2
    nodes = (np.cos((np.arange(400) + 0.5) * math.pi / 400) + 1.0) * 0.5 * top
    root = np.sqrt(nodes)
    fits = []
    for values, order in (
        (math.sqrt(2.0) * np.sin(root / 2) / root, 5),
        (math.sqrt(2.0) * np.cos(root / 2), 6),
    ):
        fit = np.polynomial.chebyshev.Chebyshev.fit(nodes, values, order - 1, domain=[0.0, top])
        fits.append([float(v) for v in fit.convert(kind=np.polynomial.Polynomial).coef])
    return fits


SIN_COEF, COS_COEF = half_angle_coefficients()


def weights_kernel(freq_ref, steer_ref, out_ref):
    channel = pl.program_id(1)
    beams = steer_ref.shape[1]
    frequency = freq_ref[channel]
    rows = steer_ref.shape[0]

    def step(index, carry):
        at = pl.ds(pl.multiple_of(index * 16, 16), 16)
        phase = np.float32(2.0 * math.pi) * (frequency * steer_ref[at, :])
        cosine, sines = sincos(phase)
        out_ref[0, at, :beams] = cosine.astype(jnp.bfloat16)
        out_ref[0, at, beams:] = sines.astype(jnp.bfloat16)
        return carry

    lax.fori_loop(0, rows // 16, step, 0)


def beam_weights(frequency, steering_t):
    antennas, beams = steering_t.shape
    channels = frequency.shape[0]
    block = min(512, antennas)
    return pl.pallas_call(
        weights_kernel,
        grid=(antennas // block, channels),
        in_specs=[
            pl.BlockSpec(memory_space=pltpu.SMEM),
            pl.BlockSpec((block, beams), lambda a, c: (a, 0)),
        ],
        out_specs=pl.BlockSpec((1, block, 2 * beams), lambda a, c: (c, a, 0)),
        out_shape=jax.ShapeDtypeStruct((channels, antennas, 2 * beams), jnp.bfloat16),
        compiler_params=pltpu.CompilerParams(vmem_limit_bytes=32 * MIB),
        cost_estimate=pl.CostEstimate(
            flops=30 * channels * antennas * beams,
            bytes_accessed=4 * channels * antennas * beams,
            transcendentals=2 * channels * antennas * beams,
        ),
        name="weights",
    )(frequency, steering_t)


def beam_kernel(wide, tm, data_ref, weight_ref, power_ref, sum_ref, gather_ref, acc_ref):
    channel = pl.program_id(0)
    groups = data_ref.shape[2]
    antennas = data_ref.shape[4]
    rows = groups * 16
    for w in range(wide):
        for m in range(tm):
            gather_ref[m * rows : (m + 1) * rows, w * antennas : (w + 1) * antennas] = data_ref[
                w * tm + m, 0
            ].reshape(rows, antennas)
    products = jnp.dot(gather_ref[...], weight_ref[0], preferred_element_type=jnp.float32)
    beams = products.shape[1] // 2
    products = products.reshape(tm * groups, 2, 8, 2 * beams)
    real_in = products[:, 0]
    imag_in = products[:, 1]
    beam_real = real_in[..., :beams] + imag_in[..., beams:]
    beam_imag = imag_in[..., :beams] - real_in[..., beams:]
    power = beam_real * beam_real + beam_imag * beam_imag
    power_ref[0] = power.reshape(tm * groups * 8, beams)
    total = jnp.sum(jnp.sum(power, axis=0), axis=(0, 1), keepdims=True)
    lane = lax.broadcasted_iota(jnp.int32, acc_ref.shape, 1)

    @pl.when(channel == 0)
    def _():
        acc_ref[...] = jnp.zeros_like(acc_ref)

    acc_ref[...] = jnp.where(lane == channel, total, acc_ref[...])

    @pl.when(channel == pl.num_programs(0) - 1)
    def _():
        sum_ref[...] = jnp.broadcast_to(acc_ref[...], sum_ref.shape)


def form_beams(received, weights, wide, tm):
    devices, channels, groups, _, antennas = received.shape
    _, antenna_full, twice = weights.shape
    frames = tm * groups * 8
    beams = twice // 2
    return pl.pallas_call(
        functools.partial(beam_kernel, wide, tm),
        grid=(channels,),
        in_specs=[
            pl.BlockSpec((devices, 1, groups, 16, antennas), lambda c: (0, c, 0, 0, 0)),
            pl.BlockSpec((1, antenna_full, twice), lambda c: (c, 0, 0)),
        ],
        out_specs=[
            pl.BlockSpec((1, frames, beams), lambda c: (c, 0, 0)),
            pl.BlockSpec((devices, 128), lambda c: (0, 0)),
        ],
        out_shape=[
            jax.ShapeDtypeStruct((channels, frames, beams), jnp.float32),
            jax.ShapeDtypeStruct((devices, 128), jnp.float32),
        ],
        scratch_shapes=[
            pltpu.VMEM((2 * frames, antenna_full), jnp.bfloat16),
            pltpu.VMEM((1, 128), jnp.float32),
        ],
        compiler_params=pltpu.CompilerParams(vmem_limit_bytes=48 * MIB),
        cost_estimate=pl.CostEstimate(
            flops=4 * channels * frames * antenna_full * twice,
            bytes_accessed=2 * channels * antenna_full * twice,
            transcendentals=0,
        ),
        name="beams",
    )(received, weights)


def level_kernel(wide, tm, reach, mask_ref, count_ref, sums_ref, power_ref, out_ref):
    channels, frames, beams = power_ref.shape
    own_beams = beams // wide
    own_frames = frames // tm
    per_row = max(1, 128 // own_beams)
    sums = sums_ref[...]
    means = []
    for c in range(channels):
        means.append(jnp.sum(jnp.sum(mask_ref[c] * sums, axis=0, keepdims=True), axis=1, keepdims=True))
    mean = jnp.concatenate(means, axis=0) / count_ref[...]
    span = own_frames + reach

    def level(f):
        value = jnp.concatenate([power_ref[c, f : f + 1, :] for c in range(channels)], axis=0)
        return (value / mean).astype(jnp.bfloat16)

    for start in range(0, frames, per_row):
        values = [level(f) for f in range(start, start + per_row)]
        for w in range(wide):
            piece = jnp.concatenate(
                [v[:, w * own_beams : (w + 1) * own_beams] for v in values], axis=1
            )
            for m in range(tm):
                for lap in (0, frames):
                    at = start + lap - m * own_frames
                    if 0 <= at < span:
                        width = min(per_row, span - at) * own_beams
                        out_ref[w * tm + m, :, at * own_beams : at * own_beams + width] = piece[
                            :, :width
                        ]


def form_levels(mask, count, sums, powers, wide, tm, reach):
    channels, frames, beams = powers.shape
    span = frames // tm + reach
    lanes = span * (beams // wide)
    return pl.pallas_call(
        functools.partial(level_kernel, wide, tm, reach),
        out_shape=jax.ShapeDtypeStruct((wide * tm, channels, lanes), jnp.bfloat16),
        compiler_params=pltpu.CompilerParams(vmem_limit_bytes=48 * MIB),
        name="levels",
    )(mask, count, sums, powers)


def search_kernel(own_frames, own_beams, width_ref, pick_ref, level_ref, out_ref, turn_ref, sum_ref):
    widths = out_ref.shape[0]
    channels, lanes = level_ref.shape
    delays = MAXDELAY + 1
    frames = own_frames + WMAX - 1
    for start in range(0, lanes, 128):
        stop = min(start + 128, lanes)
        turn_ref[start:stop, :] = level_ref[:, start:stop].T
    chunk = 8
    for start in range(0, frames, chunk):
        stop = min(start + chunk, frames)
        held = jnp.concatenate(
            [
                turn_ref[(start + d) * own_beams : (stop + d) * own_beams, :]
                for d in range(delays)
            ],
            axis=1,
        )
        value = jnp.dot(held, pick_ref[...], preferred_element_type=jnp.float32)
        sum_ref[0, start * own_beams : stop * own_beams, :] = value
    window = own_frames * own_beams
    for at in range(0, own_frames, 4):
        rows = pl.ds(at * own_beams, 4 * own_beams)
        total = sum_ref[0, rows, :]
        for lag in range(1, WMAX):
            total = total + sum_ref[0, pl.ds((at + lag) * own_beams, 4 * own_beams), :]
            sum_ref[lag, rows, :] = total
    for i in range(widths):
        expected = width_ref[i].astype(jnp.float32) * np.float32(channels)
        root = jnp.sqrt(jnp.full((1, out_ref.shape[2]), expected, jnp.float32))
        out_ref[i] = (sum_ref[width_ref[i] - 1, :window, :] - expected) / root


def search(box_widths, picks, levels, own_frames, own_beams):
    trials = picks.shape[1]
    channels, lanes = levels.shape
    widths = box_widths.shape[0]
    frames = own_frames + WMAX - 1
    return pl.pallas_call(
        functools.partial(search_kernel, own_frames, own_beams),
        in_specs=[
            pl.BlockSpec(memory_space=pltpu.SMEM),
            pl.BlockSpec(memory_space=pltpu.VMEM),
            pl.BlockSpec(memory_space=pltpu.VMEM),
        ],
        out_shape=jax.ShapeDtypeStruct((widths, own_frames * own_beams, trials), jnp.float32),
        scratch_shapes=[
            pltpu.VMEM((lanes, channels), jnp.bfloat16),
            pltpu.VMEM((WMAX, frames * own_beams, trials), jnp.float32),
        ],
        compiler_params=pltpu.CompilerParams(vmem_limit_bytes=48 * MIB),
        name="search",
    )(box_widths, picks, levels)


def exchange(value):
    return lax.all_to_all(value, AXES, split_axis=0, concat_axis=0, tiled=True)


def body(voltages, fir_taps, steering, band_widths, delays, box_widths):
    wide = lax.axis_size("wide")
    tm = lax.axis_size("tm")
    devices = wide * tm
    taps, channel_rows = fir_taps.shape
    antenna_local = voltages.shape[1]
    beam_count = steering.shape[0]
    sample_count = voltages.shape[2]
    frame_rows = sample_count // channel_rows
    total_frames = frame_rows * tm
    slots = channel_rows // devices
    own = lax.axis_index("wide") * tm + lax.axis_index("tm")
    own_ids = own * slots + jnp.arange(slots, dtype=jnp.int32)

    lookback = (taps - 1) * channel_rows
    halo = lax.ppermute(
        voltages[:, :, sample_count - lookback :], "tm", [(i, (i + 1) % tm) for i in range(tm)]
    )
    table = jnp.asarray(dft_rows(channel_rows))
    outgoing = spectra(table, voltages, voltages, fir_taps)
    outgoing = spectra(table, halo, voltages, fir_taps, outgoing)
    groups = frame_rows // 8
    received = exchange(outgoing.reshape(devices, slots * groups * 16, antenna_local))
    received = received.reshape(devices, slots, groups, 16, antenna_local)

    frequency = 1.0 + own_ids.astype(jnp.float32) / channel_rows
    weights = beam_weights(frequency, steering.T)
    powers, sums = form_beams(received, weights, wide, tm)

    starts = jnp.cumsum(band_widths) - band_widths
    ids = jnp.arange(channel_rows, dtype=jnp.int32)
    bands = jnp.sum((ids[:, None] >= starts[None, :]).astype(jnp.int32), axis=1) - 1
    own_band = jnp.sum((own_ids[:, None] >= starts[None, :]).astype(jnp.int32), axis=1) - 1
    mask = (own_band[:, None] == bands[None, :]).astype(jnp.float32)
    mask = jnp.pad(mask.reshape(slots, devices, slots), ((0, 0), (0, 0), (0, 128 - slots)))
    count = jnp.sum(
        jnp.where(
            own_band[:, None] == jnp.arange(band_widths.shape[0], dtype=jnp.int32)[None, :],
            band_widths.astype(jnp.float32)[None, :] * (total_frames * beam_count),
            0.0,
        ),
        axis=1,
        keepdims=True,
    )
    reach = MAXDELAY + WMAX - 1
    levels = form_levels(mask, count, exchange(sums), powers, wide, tm, reach)
    arrived = exchange(levels).reshape(channel_rows, levels.shape[2])

    steps = jnp.arange(MAXDELAY + 1, dtype=jnp.int32)
    picks = (delays.T[None, :, :] == steps[:, None, None]).astype(jnp.bfloat16)
    picks = picks.reshape((MAXDELAY + 1) * channel_rows, delays.shape[0])
    own_beams = beam_count // wide
    found = search(box_widths, picks, arrived, frame_rows, own_beams)
    found = found.reshape(box_widths.shape[0], frame_rows, own_beams, delays.shape[0])
    return found.transpose(3, 0, 1, 2)


def solution(mesh):
    return jax.shard_map(
        body,
        mesh=mesh,
        in_specs=(P(None, "wide", "tm"), P(), P(), P(), P(), P()),
        out_specs=P(None, None, "tm", "wide"),
        check_vma=False,
    )
```

```python
import functools
import math

import jax
import jax.numpy as jnp
import numpy as np
from jax import lax
from jax.experimental import pallas as pl
from jax.experimental.pallas import tpu as pltpu
from jax.sharding import PartitionSpec as P

MAXDELAY = 7
WMAX = 8
AXES = ("wide", "tm")
MIB = 1 << 20


def slot_parts(slots):
    late = max(1, slots // 8)
    return slots - late, late


def dft_rows(channel_rows, slots):
    positions = np.arange(channel_rows, dtype=np.int64)
    product = (positions[:, None] * positions[None, :] % channel_rows).astype(np.float32)
    angles = np.float32(2.0 * math.pi / channel_rows) * product
    cosine = np.cos(angles.astype(np.float64)).astype(np.float32)
    sines = np.sin(angles.astype(np.float64)).astype(np.float32)
    real_rows = np.concatenate([cosine.T, sines.T], axis=1)
    imag_rows = np.concatenate([-sines.T, cosine.T], axis=1)
    rows = np.stack([real_rows, imag_rows], axis=1).reshape(-1, slots, 2, 2 * channel_rows)
    first = 0
    ordered = []
    for count in slot_parts(slots):
        ordered.append(rows[:, first : first + count].reshape(-1, 2 * channel_rows))
        first += count
    return np.concatenate(ordered).astype(jnp.bfloat16)


def spectra_kernel(skip, parts, taps_ref, table_ref, past_ref, volt_ref, *rest):
    out_refs, part_ref = rest[-1 - parts : -1], rest[-1]
    taps = taps_ref.shape[0]
    width = taps_ref.shape[1]
    for inner in range(8):
        pieces = []
        for part in range(2):
            total = None
            for back in range(taps):
                if inner >= back:
                    at = (inner - back) * width
                    value = volt_ref[part, :, at : at + width]
                else:
                    at = skip + (taps - 1 + inner - back) * width
                    value = past_ref[part, :, at : at + width]
                term = taps_ref[back : back + 1, :] * value.astype(jnp.float32)
                total = term if total is None else total + term
            pieces.append(total.astype(jnp.bfloat16))
        filtered = jnp.concatenate(pieces, axis=1)
        spectrum = lax.dot_general(
            table_ref[...], filtered, (((1,), (1,)), ((), ())), preferred_element_type=jnp.float32
        )
        rows, antennas = spectrum.shape
        lanes = part_ref.shape[0] * 128
        if lanes > antennas:
            spectrum = jnp.concatenate(
                [spectrum, jnp.zeros((rows, lanes - antennas), jnp.float32)], axis=1
            )
        for half in range(lanes // 128):
            part_ref[half, pl.ds(inner, rows, stride=8), :] = spectrum[
                :, half * 128 : half * 128 + 128
            ]
    for half in range(lanes // 128):
        size = min(128, antennas - half * 128)
        first = 0
        for out_ref in out_refs:
            count = out_ref.shape[0]
            value = part_ref[half, first * 16 : (first + count) * 16].astype(jnp.bfloat16)
            value = value.reshape(count, 16, 128)
            out_ref[:, 0, :, half * 128 : half * 128 + size] = value[:, :, :size]
            first += count


def spectra(counts, table, past, voltages, fir_taps, earlier=None):
    taps, width = fir_taps.shape
    antennas = voltages.shape[1]
    groups = voltages.shape[2] // (8 * width)
    first = 1 if earlier is None else 0
    steps = groups - 1 if earlier is None else 1
    operands = [fir_taps, table, past, voltages]
    in_specs = [
        pl.BlockSpec(fir_taps.shape, lambda g: (0, 0)),
        pl.BlockSpec(table.shape, lambda g: (0, 0)),
        pl.BlockSpec((2, antennas, 4 * width), lambda g: (0, 0, 2 * g + 1))
        if earlier is None
        else pl.BlockSpec(past.shape, lambda g: (0, 0, 0)),
        pl.BlockSpec((2, antennas, 8 * width), lambda g: (0, 0, g + first)),
    ]
    if earlier is not None:
        operands.extend(earlier)
        in_specs.extend([pl.BlockSpec(memory_space=pl.ANY)] * len(counts))
    return pl.pallas_call(
        functools.partial(
            spectra_kernel, (5 - taps) * width if earlier is None else 0, len(counts)
        ),
        grid=(steps,),
        in_specs=in_specs,
        out_specs=[
            pl.BlockSpec((count, 1, 16, antennas), lambda g: (0, g + first, 0, 0))
            for count in counts
        ],
        out_shape=[
            jax.ShapeDtypeStruct((count, groups, 16, antennas), jnp.bfloat16) for count in counts
        ],
        scratch_shapes=[
            pltpu.VMEM((-(-antennas // 128), 2 * width * 8, 128), jnp.float32),
        ],
        input_output_aliases={} if earlier is None else {4 + i: i for i in range(len(counts))},
        compiler_params=pltpu.CompilerParams(vmem_limit_bytes=48 * MIB),
        cost_estimate=pl.CostEstimate(
            flops=64 * steps * antennas * width * width,
            bytes_accessed=64 * steps * antennas * width,
            transcendentals=0,
        ),
        name="spectra",
    )(*operands)


def sincos(phase):
    turns = jnp.round(phase * np.float32(1.0 / (2.0 * math.pi)))
    high = np.float32(6.28125)
    middle = np.float32(np.round((2.0 * math.pi - 6.28125) * 2.0**26) / 2.0**26)
    low = np.float32(2.0 * math.pi - 6.28125 - float(middle))
    rest = phase - turns * high
    rest = rest - turns * middle
    rest = rest - turns * low
    square = rest * rest
    s = np.float32(SIN_COEF[-1])
    for value in SIN_COEF[-2::-1]:
        s = s * square + np.float32(value)
    s = s * rest
    c = np.float32(COS_COEF[-1])
    for value in COS_COEF[-2::-1]:
        c = c * square + np.float32(value)
    return np.float32(1.0) - s * s, s * c


def half_angle_coefficients():
    top = (math.pi + 0.01) ** 2
    nodes = (np.cos((np.arange(400) + 0.5) * math.pi / 400) + 1.0) * 0.5 * top
    root = np.sqrt(nodes)
    fits = []
    for values, order in (
        (math.sqrt(2.0) * np.sin(root / 2) / root, 5),
        (math.sqrt(2.0) * np.cos(root / 2), 6),
    ):
        fit = np.polynomial.chebyshev.Chebyshev.fit(nodes, values, order - 1, domain=[0.0, top])
        fits.append([float(v) for v in fit.convert(kind=np.polynomial.Polynomial).coef])
    return fits


SIN_COEF, COS_COEF = half_angle_coefficients()


def weights_kernel(freq_ref, steer_ref, out_ref):
    channel = pl.program_id(1)
    beams = steer_ref.shape[1]
    frequency = freq_ref[channel]
    rows = steer_ref.shape[0]

    def step(index, carry):
        at = pl.ds(pl.multiple_of(index * 16, 16), 16)
        phase = np.float32(2.0 * math.pi) * (frequency * steer_ref[at, :])
        cosine, sines = sincos(phase)
        out_ref[0, at, :beams] = cosine.astype(jnp.bfloat16)
        out_ref[0, at, beams:] = sines.astype(jnp.bfloat16)
        return carry

    lax.fori_loop(0, rows // 16, step, 0)


def beam_weights(frequency, steering_t):
    antennas, beams = steering_t.shape
    channels = frequency.shape[0]
    block = min(512, antennas)
    return pl.pallas_call(
        weights_kernel,
        grid=(antennas // block, channels),
        in_specs=[
            pl.BlockSpec(memory_space=pltpu.SMEM),
            pl.BlockSpec((block, beams), lambda a, c: (a, 0)),
        ],
        out_specs=pl.BlockSpec((1, block, 2 * beams), lambda a, c: (c, a, 0)),
        out_shape=jax.ShapeDtypeStruct((channels, antennas, 2 * beams), jnp.bfloat16),
        compiler_params=pltpu.CompilerParams(vmem_limit_bytes=32 * MIB),
        cost_estimate=pl.CostEstimate(
            flops=30 * channels * antennas * beams,
            bytes_accessed=4 * channels * antennas * beams,
            transcendentals=2 * channels * antennas * beams,
        ),
        name="weights",
    )(frequency, steering_t)


def beam_kernel(wide, tm, first, before_ref, data_ref, weight_ref, power_ref, sum_ref, gather_ref, acc_ref):
    channel = pl.program_id(0)
    groups = data_ref.shape[2]
    antennas = data_ref.shape[4]
    rows = groups * 16
    for w in range(wide):
        for m in range(tm):
            gather_ref[m * rows : (m + 1) * rows, w * antennas : (w + 1) * antennas] = data_ref[
                w * tm + m, 0
            ].reshape(rows, antennas)
    products = jnp.dot(gather_ref[...], weight_ref[0], preferred_element_type=jnp.float32)
    beams = products.shape[1] // 2
    products = products.reshape(tm * groups, 2, 8, 2 * beams)
    real_in = products[:, 0]
    imag_in = products[:, 1]
    beam_real = real_in[..., :beams] + imag_in[..., beams:]
    beam_imag = imag_in[..., :beams] - real_in[..., beams:]
    power = beam_real * beam_real + beam_imag * beam_imag
    power_ref[0] = power.reshape(tm * groups * 8, beams)
    total = jnp.sum(jnp.sum(power, axis=0), axis=(0, 1), keepdims=True)
    lane = lax.broadcasted_iota(jnp.int32, acc_ref.shape, 1)

    @pl.when(channel == 0)
    def _():
        acc_ref[...] = before_ref[:1, :]

    acc_ref[...] = jnp.where(lane == channel + first, total, acc_ref[...])

    @pl.when(channel == pl.num_programs(0) - 1)
    def _():
        sum_ref[...] = jnp.broadcast_to(acc_ref[...], sum_ref.shape)


def form_beams(received, weights, before, first, wide, tm):
    devices, channels, groups, _, antennas = received.shape
    _, antenna_full, twice = weights.shape
    frames = tm * groups * 8
    beams = twice // 2
    return pl.pallas_call(
        functools.partial(beam_kernel, wide, tm, first),
        grid=(channels,),
        in_specs=[
            pl.BlockSpec((devices, 128), lambda c: (0, 0)),
            pl.BlockSpec((devices, 1, groups, 16, antennas), lambda c: (0, c, 0, 0, 0)),
            pl.BlockSpec((1, antenna_full, twice), lambda c: (c + first, 0, 0)),
        ],
        out_specs=[
            pl.BlockSpec((1, frames, beams), lambda c: (c, 0, 0)),
            pl.BlockSpec((devices, 128), lambda c: (0, 0)),
        ],
        out_shape=[
            jax.ShapeDtypeStruct((channels, frames, beams), jnp.float32),
            jax.ShapeDtypeStruct((devices, 128), jnp.float32),
        ],
        scratch_shapes=[
            pltpu.VMEM((2 * frames, antenna_full), jnp.bfloat16),
            pltpu.VMEM((1, 128), jnp.float32),
        ],
        compiler_params=pltpu.CompilerParams(vmem_limit_bytes=48 * MIB),
        cost_estimate=pl.CostEstimate(
            flops=4 * channels * frames * antenna_full * twice,
            bytes_accessed=2 * channels * antenna_full * twice,
            transcendentals=0,
        ),
        name="beams",
    )(before, received, weights)


def level_kernel(wide, tm, reach, mask_ref, count_ref, sums_ref, *refs):
    power_refs, out_ref = refs[:-1], refs[-1]
    channels = mask_ref.shape[0]
    _, frames, beams = power_refs[0].shape
    slots = [(ref, c) for ref in power_refs for c in range(ref.shape[0])]
    own_beams = beams // wide
    own_frames = frames // tm
    per_row = max(1, 128 // own_beams)
    sums = sums_ref[...]
    means = []
    for c in range(channels):
        means.append(jnp.sum(jnp.sum(mask_ref[c] * sums, axis=0, keepdims=True), axis=1, keepdims=True))
    mean = jnp.concatenate(means, axis=0) / count_ref[...]
    span = own_frames + reach

    def level(f):
        value = jnp.concatenate([ref[c, f : f + 1, :] for ref, c in slots], axis=0)
        return (value / mean).astype(jnp.bfloat16)

    for start in range(0, frames, per_row):
        values = [level(f) for f in range(start, start + per_row)]
        for w in range(wide):
            piece = jnp.concatenate(
                [v[:, w * own_beams : (w + 1) * own_beams] for v in values], axis=1
            )
            for m in range(tm):
                for lap in (0, frames):
                    at = start + lap - m * own_frames
                    if 0 <= at < span:
                        width = min(per_row, span - at) * own_beams
                        out_ref[w * tm + m, :, at * own_beams : at * own_beams + width] = piece[
                            :, :width
                        ]


def form_levels(mask, count, sums, powers, wide, tm, reach):
    channels = mask.shape[0]
    _, frames, beams = powers[0].shape
    span = frames // tm + reach
    lanes = span * (beams // wide)
    return pl.pallas_call(
        functools.partial(level_kernel, wide, tm, reach),
        out_shape=jax.ShapeDtypeStruct((wide * tm, channels, lanes), jnp.bfloat16),
        compiler_params=pltpu.CompilerParams(vmem_limit_bytes=48 * MIB),
        name="levels",
    )(mask, count, sums, *powers)


def search_kernel(own_frames, own_beams, width_ref, pick_ref, level_ref, out_ref, turn_ref, sum_ref):
    widths = out_ref.shape[0]
    channels, lanes = level_ref.shape
    delays = MAXDELAY + 1
    frames = own_frames + WMAX - 1
    for start in range(0, lanes, 128):
        stop = min(start + 128, lanes)
        turn_ref[start:stop, :] = level_ref[:, start:stop].T
    chunk = 8
    for start in range(0, frames, chunk):
        stop = min(start + chunk, frames)
        held = jnp.concatenate(
            [
                turn_ref[(start + d) * own_beams : (stop + d) * own_beams, :]
                for d in range(delays)
            ],
            axis=1,
        )
        value = jnp.dot(held, pick_ref[...], preferred_element_type=jnp.float32)
        sum_ref[0, start * own_beams : stop * own_beams, :] = value
    window = own_frames * own_beams
    for at in range(0, own_frames, 4):
        rows = pl.ds(at * own_beams, 4 * own_beams)
        total = sum_ref[0, rows, :]
        for lag in range(1, WMAX):
            total = total + sum_ref[0, pl.ds((at + lag) * own_beams, 4 * own_beams), :]
            sum_ref[lag, rows, :] = total
    for i in range(widths):
        expected = width_ref[i].astype(jnp.float32) * np.float32(channels)
        root = jnp.sqrt(jnp.full((1, out_ref.shape[2]), expected, jnp.float32))
        out_ref[i] = (sum_ref[width_ref[i] - 1, :window, :] - expected) / root


def search(box_widths, picks, levels, own_frames, own_beams):
    trials = picks.shape[1]
    channels, lanes = levels.shape
    widths = box_widths.shape[0]
    frames = own_frames + WMAX - 1
    return pl.pallas_call(
        functools.partial(search_kernel, own_frames, own_beams),
        in_specs=[
            pl.BlockSpec(memory_space=pltpu.SMEM),
            pl.BlockSpec(memory_space=pltpu.VMEM),
            pl.BlockSpec(memory_space=pltpu.VMEM),
        ],
        out_shape=jax.ShapeDtypeStruct((widths, own_frames * own_beams, trials), jnp.float32),
        scratch_shapes=[
            pltpu.VMEM((lanes, channels), jnp.bfloat16),
            pltpu.VMEM((WMAX, frames * own_beams, trials), jnp.float32),
        ],
        compiler_params=pltpu.CompilerParams(vmem_limit_bytes=48 * MIB),
        name="search",
    )(box_widths, picks, levels)


def exchange(value):
    return lax.all_to_all(value, AXES, split_axis=0, concat_axis=0, tiled=True)


def body(voltages, fir_taps, steering, band_widths, delays, box_widths):
    wide = lax.axis_size("wide")
    tm = lax.axis_size("tm")
    devices = wide * tm
    taps, channel_rows = fir_taps.shape
    antenna_local = voltages.shape[1]
    beam_count = steering.shape[0]
    sample_count = voltages.shape[2]
    frame_rows = sample_count // channel_rows
    total_frames = frame_rows * tm
    slots = channel_rows // devices
    own = lax.axis_index("wide") * tm + lax.axis_index("tm")
    own_ids = own * slots + jnp.arange(slots, dtype=jnp.int32)

    lookback = (taps - 1) * channel_rows
    halo = lax.ppermute(
        voltages[:, :, sample_count - lookback :], "tm", [(i, (i + 1) % tm) for i in range(tm)]
    )
    parts = slot_parts(slots)
    counts = [devices * part for part in parts]
    table = pltpu.with_memory_space_constraint(
        jnp.asarray(dft_rows(channel_rows, slots)), pltpu.HBM
    )
    fir_taps = pltpu.with_memory_space_constraint(fir_taps, pltpu.HBM)
    outgoing = spectra(counts, table, voltages, voltages, fir_taps)
    early, tail = spectra(counts, table, halo, voltages, fir_taps, outgoing)
    groups = frame_rows // 8

    def arrive(piece, part):
        received = exchange(piece.reshape(devices, part * groups * 16, antenna_local))
        return received.reshape(devices, part, groups, 16, antenna_local)

    frequency = 1.0 + own_ids.astype(jnp.float32) / channel_rows
    early, frequency, steering = lax.optimization_barrier((early, frequency, steering))
    weights = beam_weights(frequency, steering.T)
    early = arrive(early, parts[0])
    early, tail, weights = lax.optimization_barrier((early, tail, weights))
    sums = jnp.zeros((devices, 128), jnp.float32)
    power, sums = form_beams(early, weights, sums, 0, wide, tm)
    late, sums = form_beams(arrive(tail, parts[1]), weights, sums, parts[0], wide, tm)
    powers = [power, late]

    starts = jnp.cumsum(band_widths) - band_widths
    ids = jnp.arange(channel_rows, dtype=jnp.int32)
    bands = jnp.sum((ids[:, None] >= starts[None, :]).astype(jnp.int32), axis=1) - 1
    own_band = jnp.sum((own_ids[:, None] >= starts[None, :]).astype(jnp.int32), axis=1) - 1
    mask = (own_band[:, None] == bands[None, :]).astype(jnp.float32)
    mask = jnp.pad(mask.reshape(slots, devices, slots), ((0, 0), (0, 0), (0, 128 - slots)))
    count = jnp.sum(
        jnp.where(
            own_band[:, None] == jnp.arange(band_widths.shape[0], dtype=jnp.int32)[None, :],
            band_widths.astype(jnp.float32)[None, :] * (total_frames * beam_count),
            0.0,
        ),
        axis=1,
        keepdims=True,
    )
    reach = MAXDELAY + WMAX - 1
    levels = form_levels(mask, count, exchange(sums), powers, wide, tm, reach)
    arrived = exchange(levels).reshape(channel_rows, levels.shape[2])

    steps = jnp.arange(MAXDELAY + 1, dtype=jnp.int32)
    picks = (delays.T[None, :, :] == steps[:, None, None]).astype(jnp.bfloat16)
    picks = picks.reshape((MAXDELAY + 1) * channel_rows, delays.shape[0])
    own_beams = beam_count // wide
    found = search(box_widths, picks, arrived, frame_rows, own_beams)
    found = found.reshape(box_widths.shape[0], frame_rows, own_beams, delays.shape[0])
    return found.transpose(3, 0, 1, 2)


def solution(mesh):
    return jax.shard_map(
        body,
        mesh=mesh,
        in_specs=(P(None, "wide", "tm"), P(), P(), P(), P(), P()),
        out_specs=P(None, None, "tm", "wide"),
        check_vma=False,
    )
```

```python
import functools
import math

import jax
import jax.numpy as jnp
import numpy as np
from jax import lax
from jax.experimental import pallas as pl
from jax.experimental.pallas import tpu as pltpu
from jax.sharding import PartitionSpec as P

MAXDELAY = 7
WMAX = 8
AXES = ("wide", "tm")
MIB = 1 << 20


def slot_parts(slots):
    late = max(1, slots // 8)
    return slots - late, late


def dft_rows(channel_rows, slots):
    positions = np.arange(channel_rows, dtype=np.int64)
    product = (positions[:, None] * positions[None, :] % channel_rows).astype(np.float32)
    angles = np.float32(2.0 * math.pi / channel_rows) * product
    cosine = np.cos(angles.astype(np.float64)).astype(np.float32)
    sines = np.sin(angles.astype(np.float64)).astype(np.float32)
    real_rows = np.concatenate([cosine.T, sines.T], axis=1)
    imag_rows = np.concatenate([-sines.T, cosine.T], axis=1)
    rows = np.stack([real_rows, imag_rows], axis=1).reshape(-1, slots, 2, 2 * channel_rows)
    first = 0
    ordered = []
    for count in slot_parts(slots):
        ordered.append(rows[:, first : first + count].reshape(-1, 2 * channel_rows))
        first += count
    return np.concatenate(ordered).astype(jnp.bfloat16)


def spectra_kernel(skip, parts, taps_ref, table_ref, past_ref, volt_ref, *rest):
    out_refs, part_ref = rest[-1 - parts : -1], rest[-1]
    taps = taps_ref.shape[0]
    width = taps_ref.shape[1]
    for inner in range(8):
        pieces = []
        for part in range(2):
            total = None
            for back in range(taps):
                if inner >= back:
                    at = (inner - back) * width
                    value = volt_ref[part, :, at : at + width]
                else:
                    at = skip + (taps - 1 + inner - back) * width
                    value = past_ref[part, :, at : at + width]
                term = taps_ref[back : back + 1, :] * value.astype(jnp.float32)
                total = term if total is None else total + term
            pieces.append(total.astype(jnp.bfloat16))
        filtered = jnp.concatenate(pieces, axis=1)
        spectrum = lax.dot_general(
            table_ref[...], filtered, (((1,), (1,)), ((), ())), preferred_element_type=jnp.float32
        )
        rows, antennas = spectrum.shape
        lanes = part_ref.shape[0] * 128
        if lanes > antennas:
            spectrum = jnp.concatenate(
                [spectrum, jnp.zeros((rows, lanes - antennas), jnp.float32)], axis=1
            )
        for half in range(lanes // 128):
            part_ref[half, pl.ds(inner, rows, stride=8), :] = spectrum[
                :, half * 128 : half * 128 + 128
            ]
    for half in range(lanes // 128):
        size = min(128, antennas - half * 128)
        first = 0
        for out_ref in out_refs:
            count = out_ref.shape[0]
            value = part_ref[half, first * 16 : (first + count) * 16].astype(jnp.bfloat16)
            value = value.reshape(count, 16, 128)
            out_ref[:, 0, :, half * 128 : half * 128 + size] = value[:, :, :size]
            first += count


def spectra(counts, table, past, voltages, fir_taps, earlier=None):
    taps, width = fir_taps.shape
    antennas = voltages.shape[1]
    groups = voltages.shape[2] // (8 * width)
    first = 1 if earlier is None else 0
    steps = groups - 1 if earlier is None else 1
    operands = [fir_taps, table, past, voltages]
    in_specs = [
        pl.BlockSpec(fir_taps.shape, lambda g: (0, 0)),
        pl.BlockSpec(table.shape, lambda g: (0, 0)),
        pl.BlockSpec((2, antennas, 4 * width), lambda g: (0, 0, 2 * g + 1))
        if earlier is None
        else pl.BlockSpec(past.shape, lambda g: (0, 0, 0)),
        pl.BlockSpec((2, antennas, 8 * width), lambda g: (0, 0, g + first)),
    ]
    if earlier is not None:
        operands.extend(earlier)
        in_specs.extend([pl.BlockSpec(memory_space=pl.ANY)] * len(counts))
    return pl.pallas_call(
        functools.partial(
            spectra_kernel, (5 - taps) * width if earlier is None else 0, len(counts)
        ),
        grid=(steps,),
        in_specs=in_specs,
        out_specs=[
            pl.BlockSpec((count, 1, 16, antennas), lambda g: (0, g + first, 0, 0))
            for count in counts
        ],
        out_shape=[
            jax.ShapeDtypeStruct((count, groups, 16, antennas), jnp.bfloat16) for count in counts
        ],
        scratch_shapes=[
            pltpu.VMEM((-(-antennas // 128), 2 * width * 8, 128), jnp.float32),
        ],
        input_output_aliases={} if earlier is None else {4 + i: i for i in range(len(counts))},
        compiler_params=pltpu.CompilerParams(vmem_limit_bytes=48 * MIB),
        cost_estimate=pl.CostEstimate(
            flops=64 * steps * antennas * width * width,
            bytes_accessed=64 * steps * antennas * width,
            transcendentals=0,
        ),
        name="spectra",
    )(*operands)


def sincos(phase):
    turns = jnp.round(phase * np.float32(1.0 / (2.0 * math.pi)))
    high = np.float32(6.28125)
    middle = np.float32(np.round((2.0 * math.pi - 6.28125) * 2.0**26) / 2.0**26)
    low = np.float32(2.0 * math.pi - 6.28125 - float(middle))
    rest = phase - turns * high
    rest = rest - turns * middle
    rest = rest - turns * low
    square = rest * rest
    s = np.float32(SIN_COEF[-1])
    for value in SIN_COEF[-2::-1]:
        s = s * square + np.float32(value)
    s = s * rest
    c = np.float32(COS_COEF[-1])
    for value in COS_COEF[-2::-1]:
        c = c * square + np.float32(value)
    return np.float32(1.0) - s * s, s * c


def half_angle_coefficients():
    top = (math.pi + 0.01) ** 2
    nodes = (np.cos((np.arange(400) + 0.5) * math.pi / 400) + 1.0) * 0.5 * top
    root = np.sqrt(nodes)
    fits = []
    for values, order in (
        (math.sqrt(2.0) * np.sin(root / 2) / root, 5),
        (math.sqrt(2.0) * np.cos(root / 2), 6),
    ):
        fit = np.polynomial.chebyshev.Chebyshev.fit(nodes, values, order - 1, domain=[0.0, top])
        fits.append([float(v) for v in fit.convert(kind=np.polynomial.Polynomial).coef])
    return fits


SIN_COEF, COS_COEF = half_angle_coefficients()


def weights_kernel(freq_ref, steer_ref, out_ref):
    channel = pl.program_id(1)
    beams = steer_ref.shape[1]
    frequency = freq_ref[channel]
    rows = steer_ref.shape[0]

    def step(index, carry):
        at = pl.ds(pl.multiple_of(index * 16, 16), 16)
        phase = np.float32(2.0 * math.pi) * (frequency * steer_ref[at, :])
        cosine, sines = sincos(phase)
        out_ref[0, at, :beams] = cosine.astype(jnp.bfloat16)
        out_ref[0, at, beams:] = sines.astype(jnp.bfloat16)
        return carry

    lax.fori_loop(0, rows // 16, step, 0)


def beam_weights(frequency, steering_t):
    antennas, beams = steering_t.shape
    channels = frequency.shape[0]
    block = min(512, antennas)
    return pl.pallas_call(
        weights_kernel,
        grid=(antennas // block, channels),
        in_specs=[
            pl.BlockSpec(memory_space=pltpu.SMEM),
            pl.BlockSpec((block, beams), lambda a, c: (a, 0)),
        ],
        out_specs=pl.BlockSpec((1, block, 2 * beams), lambda a, c: (c, a, 0)),
        out_shape=jax.ShapeDtypeStruct((channels, antennas, 2 * beams), jnp.bfloat16),
        compiler_params=pltpu.CompilerParams(vmem_limit_bytes=32 * MIB),
        cost_estimate=pl.CostEstimate(
            flops=30 * channels * antennas * beams,
            bytes_accessed=4 * channels * antennas * beams,
            transcendentals=2 * channels * antennas * beams,
        ),
        name="weights",
    )(frequency, steering_t)


def beam_kernel(wide, tm, first, before_ref, data_ref, weight_ref, power_ref, sum_ref, gather_ref, acc_ref):
    channel = pl.program_id(0)
    groups = data_ref.shape[2]
    antennas = data_ref.shape[4]
    rows = groups * 16
    for w in range(wide):
        for m in range(tm):
            gather_ref[m * rows : (m + 1) * rows, w * antennas : (w + 1) * antennas] = data_ref[
                w * tm + m, 0
            ].reshape(rows, antennas)
    products = jnp.dot(gather_ref[...], weight_ref[0], preferred_element_type=jnp.float32)
    beams = products.shape[1] // 2
    products = products.reshape(tm * groups, 2, 8, 2 * beams)
    real_in = products[:, 0]
    imag_in = products[:, 1]
    beam_real = real_in[..., :beams] + imag_in[..., beams:]
    beam_imag = imag_in[..., :beams] - real_in[..., beams:]
    power = beam_real * beam_real + beam_imag * beam_imag
    power_ref[0] = power.reshape(tm * groups * 8, beams)
    total = jnp.sum(jnp.sum(power, axis=0), axis=(0, 1), keepdims=True)
    lane = lax.broadcasted_iota(jnp.int32, acc_ref.shape, 1)

    @pl.when(channel == 0)
    def _():
        acc_ref[...] = before_ref[:1, :]

    acc_ref[...] = jnp.where(lane == channel + first, total, acc_ref[...])

    @pl.when(channel == pl.num_programs(0) - 1)
    def _():
        sum_ref[...] = jnp.broadcast_to(acc_ref[...], sum_ref.shape)


def form_beams(received, weights, before, first, wide, tm):
    devices, channels, groups, _, antennas = received.shape
    _, antenna_full, twice = weights.shape
    frames = tm * groups * 8
    beams = twice // 2
    return pl.pallas_call(
        functools.partial(beam_kernel, wide, tm, first),
        grid=(channels,),
        in_specs=[
            pl.BlockSpec((devices, 128), lambda c: (0, 0)),
            pl.BlockSpec((devices, 1, groups, 16, antennas), lambda c: (0, c, 0, 0, 0)),
            pl.BlockSpec((1, antenna_full, twice), lambda c: (c + first, 0, 0)),
        ],
        out_specs=[
            pl.BlockSpec((1, frames, beams), lambda c: (c, 0, 0)),
            pl.BlockSpec((devices, 128), lambda c: (0, 0)),
        ],
        out_shape=[
            jax.ShapeDtypeStruct((channels, frames, beams), jnp.float32),
            jax.ShapeDtypeStruct((devices, 128), jnp.float32),
        ],
        scratch_shapes=[
            pltpu.VMEM((2 * frames, antenna_full), jnp.bfloat16),
            pltpu.VMEM((1, 128), jnp.float32),
        ],
        compiler_params=pltpu.CompilerParams(vmem_limit_bytes=48 * MIB),
        cost_estimate=pl.CostEstimate(
            flops=4 * channels * frames * antenna_full * twice,
            bytes_accessed=2 * channels * antenna_full * twice,
            transcendentals=0,
        ),
        name="beams",
    )(before, received, weights)


def level_kernel(wide, tm, mask_ref, count_ref, sums_ref, *refs):
    power_refs, out_ref = refs[:-1], refs[-1]
    channels = mask_ref.shape[0]
    _, frames, beams = power_refs[0].shape
    slots = [(ref, c) for ref in power_refs for c in range(ref.shape[0])]
    own_beams = beams // wide
    own_frames = frames // tm
    per_row = max(1, 128 // own_beams)
    sums = sums_ref[...]
    means = []
    for c in range(channels):
        means.append(jnp.sum(jnp.sum(mask_ref[c] * sums, axis=0, keepdims=True), axis=1, keepdims=True))
    mean = jnp.concatenate(means, axis=0) / count_ref[...]

    def level(f):
        value = jnp.concatenate([ref[c, f : f + 1, :] for ref, c in slots], axis=0)
        return (value / mean).astype(jnp.bfloat16)

    for start in range(0, frames, per_row):
        values = [level(f) for f in range(start, start + per_row)]
        for w in range(wide):
            piece = jnp.concatenate(
                [v[:, w * own_beams : (w + 1) * own_beams] for v in values], axis=1
            )
            m, at = divmod(start, own_frames)
            at *= own_beams
            out_ref[w * tm + m, :, at : at + per_row * own_beams] = piece


def form_levels(mask, count, sums, powers, wide, tm):
    channels = mask.shape[0]
    _, frames, beams = powers[0].shape
    lanes = frames // tm * (beams // wide)
    return pl.pallas_call(
        functools.partial(level_kernel, wide, tm),
        out_shape=jax.ShapeDtypeStruct((wide * tm, channels, lanes), jnp.bfloat16),
        compiler_params=pltpu.CompilerParams(vmem_limit_bytes=48 * MIB),
        name="levels",
    )(mask, count, sums, *powers)


def turn(source_ref, lane, lanes, target_ref, row):
    for start in range(0, lanes, 128):
        size = min(128, lanes - start)
        piece = source_ref[:, lane + start : lane + start + size].T
        target_ref[row + start : row + start + size, :] = piece


def dedisperse(turn_ref, pick_ref, sum_ref, row, frames, beams):
    chunk = 7
    for start in range(0, frames, chunk):
        stop = min(start + chunk, frames)
        held = jnp.concatenate(
            [
                turn_ref[(start + d) * beams : (stop + d) * beams, :]
                for d in range(MAXDELAY + 1)
            ],
            axis=1,
        )
        sum_ref[0, row + start * beams : row + stop * beams, :] = jnp.dot(
            held, pick_ref[...], preferred_element_type=jnp.float32
        )


def boxcars(channels, width_ref, sum_ref, stage_ref, out_ref, sems, row, beams):
    widths, rows, _ = stage_ref.shape
    for at in range(0, rows, 2 * beams):
        total = sum_ref[0, at : at + 2 * beams, :]
        for lag in range(1, WMAX):
            begin = at + lag * beams
            total = total + sum_ref[0, begin : begin + 2 * beams, :]
            sum_ref[lag, at : at + 2 * beams, :] = total
    copies = []
    for i in range(widths):
        expected = width_ref[i].astype(jnp.float32) * np.float32(channels)
        root = jnp.sqrt(jnp.full((1, stage_ref.shape[2]), expected, jnp.float32))
        stage_ref[i] = (sum_ref[width_ref[i] - 1, :rows, :] - expected) / root
        copy = pltpu.make_async_copy(
            stage_ref.at[i], out_ref.at[i, pl.ds(row, rows)], sems.at[i]
        )
        copy.start()
        copies.append(copy)
    for copy in copies:
        copy.wait()


def search_early_kernel(
    beams, width_ref, pick_ref, level_ref, out_ref, kept_ref, turn_ref, sum_ref, stage_ref, sems
):
    channels, lanes = level_ref.shape
    turn(level_ref, 0, lanes, turn_ref, 0)
    known = sum_ref.shape[1]
    dedisperse(turn_ref, pick_ref, sum_ref, 0, known // beams, beams)
    kept_ref[...] = sum_ref[0, known - kept_ref.shape[0] :, :]
    boxcars(channels, width_ref, sum_ref, stage_ref, out_ref, sems, 0, beams)


def search_late_kernel(
    beams, width_ref, pick_ref, level_ref, halo_ref, kept_ref, given_ref, out_ref, turn_ref,
    sum_ref, stage_ref, sems,
):
    channels, lanes = level_ref.shape
    held = MAXDELAY * beams
    turn(level_ref, lanes - held, held, turn_ref, 0)
    turn(halo_ref, 0, halo_ref.shape[1], turn_ref, held)
    kept = kept_ref.shape[0]
    sum_ref[0, :kept, :] = kept_ref[...]
    dedisperse(turn_ref, pick_ref, sum_ref, kept, sum_ref.shape[1] // beams - WMAX + 1, beams)
    row = lanes - stage_ref.shape[1]
    boxcars(channels, width_ref, sum_ref, stage_ref, out_ref, sems, row, beams)


def search(box_widths, picks, levels, beams):
    trials = picks.shape[1]
    channels, lanes = levels.shape
    widths = box_widths.shape[0]
    lags = WMAX - 1
    frames = lanes // beams
    known = frames - MAXDELAY
    early = known - lags
    late = frames - early
    whole = pl.BlockSpec(memory_space=pltpu.VMEM)
    params = pltpu.CompilerParams(vmem_limit_bytes=32 * MIB)
    found, kept = pl.pallas_call(
        functools.partial(search_early_kernel, beams),
        in_specs=[pl.BlockSpec(memory_space=pltpu.SMEM), whole, whole],
        out_specs=[pl.BlockSpec(memory_space=pl.ANY), whole],
        out_shape=[
            jax.ShapeDtypeStruct((widths, lanes, trials), jnp.float32),
            jax.ShapeDtypeStruct((lags * beams, trials), jnp.float32),
        ],
        scratch_shapes=[
            pltpu.VMEM((lanes, channels), jnp.bfloat16),
            pltpu.VMEM((WMAX, known * beams, trials), jnp.float32),
            pltpu.VMEM((widths, early * beams, trials), jnp.float32),
            pltpu.SemaphoreType.DMA((widths,)),
        ],
        compiler_params=params,
        name="search_early",
    )(box_widths, picks, levels)
    blocks = lax.axis_size("tm")
    halo = lax.ppermute(
        levels[:, : (MAXDELAY + lags) * beams], "tm", [(i, (i - 1) % blocks) for i in range(blocks)]
    )
    return pl.pallas_call(
        functools.partial(search_late_kernel, beams),
        in_specs=[
            pl.BlockSpec(memory_space=pltpu.SMEM),
            whole,
            whole,
            whole,
            whole,
            pl.BlockSpec(memory_space=pl.ANY),
        ],
        out_specs=pl.BlockSpec(memory_space=pl.ANY),
        out_shape=jax.ShapeDtypeStruct((widths, lanes, trials), jnp.float32),
        scratch_shapes=[
            pltpu.VMEM(((MAXDELAY + MAXDELAY + lags) * beams, channels), jnp.bfloat16),
            pltpu.VMEM((WMAX, (late + lags) * beams, trials), jnp.float32),
            pltpu.VMEM((widths, late * beams, trials), jnp.float32),
            pltpu.SemaphoreType.DMA((widths,)),
        ],
        input_output_aliases={5: 0},
        compiler_params=params,
        name="search_late",
    )(box_widths, picks, levels, halo, kept, found)


def exchange(value):
    return lax.all_to_all(value, AXES, split_axis=0, concat_axis=0, tiled=True)


def body(voltages, fir_taps, steering, band_widths, delays, box_widths):
    wide = lax.axis_size("wide")
    tm = lax.axis_size("tm")
    devices = wide * tm
    taps, channel_rows = fir_taps.shape
    antenna_local = voltages.shape[1]
    beam_count = steering.shape[0]
    sample_count = voltages.shape[2]
    frame_rows = sample_count // channel_rows
    total_frames = frame_rows * tm
    slots = channel_rows // devices
    own = lax.axis_index("wide") * tm + lax.axis_index("tm")
    own_ids = own * slots + jnp.arange(slots, dtype=jnp.int32)

    lookback = (taps - 1) * channel_rows
    halo = lax.ppermute(
        voltages[:, :, sample_count - lookback :], "tm", [(i, (i + 1) % tm) for i in range(tm)]
    )
    parts = slot_parts(slots)
    counts = [devices * part for part in parts]
    table = pltpu.with_memory_space_constraint(
        jnp.asarray(dft_rows(channel_rows, slots)), pltpu.HBM
    )
    fir_taps = pltpu.with_memory_space_constraint(fir_taps, pltpu.HBM)
    outgoing = spectra(counts, table, voltages, voltages, fir_taps)
    early, tail = spectra(counts, table, halo, voltages, fir_taps, outgoing)
    groups = frame_rows // 8

    def arrive(piece, part):
        received = exchange(piece.reshape(devices, part * groups * 16, antenna_local))
        return received.reshape(devices, part, groups, 16, antenna_local)

    frequency = 1.0 + own_ids.astype(jnp.float32) / channel_rows
    early, frequency, steering = lax.optimization_barrier((early, frequency, steering))
    weights = beam_weights(frequency, steering.T)
    early = arrive(early, parts[0])
    early, tail, weights = lax.optimization_barrier((early, tail, weights))
    sums = jnp.zeros((devices, 128), jnp.float32)
    power, sums = form_beams(early, weights, sums, 0, wide, tm)
    late, sums = form_beams(arrive(tail, parts[1]), weights, sums, parts[0], wide, tm)
    powers = [power, late]

    starts = jnp.cumsum(band_widths) - band_widths
    ids = jnp.arange(channel_rows, dtype=jnp.int32)
    bands = jnp.sum((ids[:, None] >= starts[None, :]).astype(jnp.int32), axis=1) - 1
    own_band = jnp.sum((own_ids[:, None] >= starts[None, :]).astype(jnp.int32), axis=1) - 1
    mask = (own_band[:, None] == bands[None, :]).astype(jnp.float32)
    mask = jnp.pad(mask.reshape(slots, devices, slots), ((0, 0), (0, 0), (0, 128 - slots)))
    count = jnp.sum(
        jnp.where(
            own_band[:, None] == jnp.arange(band_widths.shape[0], dtype=jnp.int32)[None, :],
            band_widths.astype(jnp.float32)[None, :] * (total_frames * beam_count),
            0.0,
        ),
        axis=1,
        keepdims=True,
    )
    levels = form_levels(mask, count, exchange(sums), powers, wide, tm)
    arrived = exchange(levels).reshape(channel_rows, levels.shape[2])

    steps = jnp.arange(MAXDELAY + 1, dtype=jnp.int32)
    picks = (delays.T[None, :, :] == steps[:, None, None]).astype(jnp.bfloat16)
    picks = picks.reshape((MAXDELAY + 1) * channel_rows, delays.shape[0])
    own_beams = beam_count // wide
    found = search(box_widths, picks, arrived, own_beams)
    found = found.reshape(box_widths.shape[0], frame_rows, own_beams, delays.shape[0])
    return found.transpose(3, 0, 1, 2)


def solution(mesh):
    return jax.shard_map(
        body,
        mesh=mesh,
        in_specs=(P(None, "wide", "tm"), P(), P(), P(), P(), P()),
        out_specs=P(None, None, "tm", "wide"),
        check_vma=False,
    )
```

```python
import functools
import math

import jax
import jax.numpy as jnp
import numpy as np
from jax import lax
from jax.experimental import pallas as pl
from jax.experimental.pallas import tpu as pltpu
from jax.sharding import PartitionSpec as P

MAXDELAY = 7
WMAX = 8
AXES = ("wide", "tm")
MIB = 1 << 20


def slot_parts(slots):
    late = max(1, slots // 8)
    return slots - late, late


def dft_rows(channel_rows, slots):
    positions = np.arange(channel_rows, dtype=np.int64)
    product = (positions[:, None] * positions[None, :] % channel_rows).astype(np.float32)
    angles = np.float32(2.0 * math.pi / channel_rows) * product
    cosine = np.cos(angles.astype(np.float64)).astype(np.float32)
    sines = np.sin(angles.astype(np.float64)).astype(np.float32)
    real_rows = np.concatenate([cosine.T, sines.T], axis=1)
    imag_rows = np.concatenate([-sines.T, cosine.T], axis=1)
    rows = np.stack([real_rows, imag_rows], axis=1).reshape(-1, slots, 2, 2 * channel_rows)
    first = 0
    ordered = []
    for count in slot_parts(slots):
        ordered.append(rows[:, first : first + count].reshape(-1, 2 * channel_rows))
        first += count
    return np.concatenate(ordered).astype(jnp.bfloat16)


def transform(inners, skip, taps_ref, table_ref, past_ref, volt_ref, part_ref):
    taps = taps_ref.shape[0]
    width = taps_ref.shape[1]
    for inner in inners:
        pieces = []
        for part in range(2):
            total = None
            for back in range(taps):
                if inner >= back:
                    at = (inner - back) * width
                    value = volt_ref[part, :, at : at + width]
                else:
                    at = skip + (taps - 1 + inner - back) * width
                    value = past_ref[part, :, at : at + width]
                term = taps_ref[back : back + 1, :] * value.astype(jnp.float32)
                total = term if total is None else total + term
            pieces.append(total.astype(jnp.bfloat16))
        filtered = jnp.concatenate(pieces, axis=1)
        spectrum = lax.dot_general(
            table_ref[...], filtered, (((1,), (1,)), ((), ())), preferred_element_type=jnp.float32
        )
        rows, antennas = spectrum.shape
        lanes = part_ref.shape[0] * 128
        if lanes > antennas:
            spectrum = jnp.concatenate(
                [spectrum, jnp.zeros((rows, lanes - antennas), jnp.float32)], axis=1
            )
        for half in range(lanes // 128):
            part_ref[half, pl.ds(inner, rows, stride=8), :] = spectrum[
                :, half * 128 : half * 128 + 128
            ]


def write_out(part_ref, out_refs, kept_ref=None, fresh=8):
    antennas = out_refs[0].shape[3]
    for half in range(part_ref.shape[0]):
        size = min(128, antennas - half * 128)
        first = 0
        for out_ref in out_refs:
            count = out_ref.shape[0]
            value = part_ref[half, first * 16 : (first + count) * 16]
            if kept_ref is not None:
                kept = kept_ref[half, first * 16 : (first + count) * 16]
                frame = lax.broadcasted_iota(jnp.int32, value.shape, 0) % 8
                value = jnp.where(frame < fresh, value, kept)
            value = value.astype(jnp.bfloat16).reshape(count, 16, 128)
            out_ref[:, 0, :, half * 128 : half * 128 + size] = value[:, :, :size]
            first += count


def spectra_kernel(skip, taps_ref, table_ref, past_ref, volt_ref, *rest):
    out_refs, kept_ref, part_ref = rest[:-2], rest[-2], rest[-1]
    taps = taps_ref.shape[0]

    @pl.when(pl.program_id(0) == 0)
    def _():
        transform(range(taps - 1, 8), 0, taps_ref, table_ref, past_ref, volt_ref, kept_ref)

    @pl.when(pl.program_id(0) > 0)
    def _():
        transform(range(8), skip, taps_ref, table_ref, past_ref, volt_ref, part_ref)
        write_out(part_ref, out_refs)


def spectra_first_kernel(taps_ref, table_ref, past_ref, volt_ref, kept_ref, *rest):
    count = (len(rest) - 1) // 2
    out_refs, part_ref = rest[count:-1], rest[-1]
    fresh = taps_ref.shape[0] - 1
    transform(range(fresh), 0, taps_ref, table_ref, past_ref, volt_ref, part_ref)
    write_out(part_ref, out_refs, kept_ref, fresh)


def spectra(counts, table, halo, voltages, fir_taps):
    taps, width = fir_taps.shape
    antennas = voltages.shape[1]
    groups = voltages.shape[2] // (8 * width)
    part = pltpu.VMEM((-(-antennas // 128), 2 * width * 8, 128), jnp.float32)
    shapes = [pltpu.HBM((count, groups, 16, antennas), jnp.bfloat16) for count in counts]

    def blocks(place):
        return [pl.BlockSpec((count, 1, 16, antennas), place) for count in counts]

    def cost(frames):
        return pl.CostEstimate(
            flops=8 * frames * antennas * width * width,
            bytes_accessed=8 * frames * antennas * width,
            transcendentals=0,
        )

    common = [
        pl.BlockSpec(fir_taps.shape, lambda g: (0, 0)),
        pl.BlockSpec(table.shape, lambda g: (0, 0)),
    ]
    *outgoing, kept = pl.pallas_call(
        functools.partial(spectra_kernel, (5 - taps) * width),
        grid=(groups,),
        in_specs=common
        + [
            pl.BlockSpec((2, antennas, 4 * width), lambda g: (0, 0, jnp.maximum(2 * g - 1, 1))),
            pl.BlockSpec((2, antennas, 8 * width), lambda g: (0, 0, g)),
        ],
        out_specs=blocks(lambda g: (0, jnp.maximum(g, 1), 0, 0))
        + [pl.BlockSpec(memory_space=pltpu.VMEM)],
        out_shape=shapes + [part],
        scratch_shapes=[part],
        compiler_params=pltpu.CompilerParams(vmem_limit_bytes=40 * MIB),
        cost_estimate=cost(8 * groups),
        name="spectra",
    )(fir_taps, table, voltages, voltages)
    kept = pltpu.with_memory_space_constraint(kept, pltpu.VMEM)
    return pl.pallas_call(
        spectra_first_kernel,
        grid=(1,),
        in_specs=common
        + [
            pl.BlockSpec(halo.shape, lambda g: (0, 0, 0)),
            pl.BlockSpec((2, antennas, 4 * width), lambda g: (0, 0, 0)),
            pl.BlockSpec(memory_space=pltpu.VMEM),
        ]
        + [pl.BlockSpec(memory_space=pl.ANY)] * len(counts),
        out_specs=blocks(lambda g: (0, 0, 0, 0)),
        out_shape=shapes,
        scratch_shapes=[part],
        input_output_aliases={5 + i: i for i in range(len(counts))},
        compiler_params=pltpu.CompilerParams(vmem_limit_bytes=32 * MIB),
        cost_estimate=cost(taps - 1),
        name="spectra_first",
    )(fir_taps, table, halo, voltages, kept, *outgoing)


def sincos(phase):
    turns = jnp.round(phase * np.float32(1.0 / (2.0 * math.pi)))
    high = np.float32(6.28125)
    middle = np.float32(np.round((2.0 * math.pi - 6.28125) * 2.0**26) / 2.0**26)
    low = np.float32(2.0 * math.pi - 6.28125 - float(middle))
    rest = phase - turns * high
    rest = rest - turns * middle
    rest = rest - turns * low
    square = rest * rest
    s = np.float32(SIN_COEF[-1])
    for value in SIN_COEF[-2::-1]:
        s = s * square + np.float32(value)
    s = s * rest
    c = np.float32(COS_COEF[-1])
    for value in COS_COEF[-2::-1]:
        c = c * square + np.float32(value)
    return np.float32(1.0) - s * s, s * c


def half_angle_coefficients():
    top = (math.pi + 0.01) ** 2
    nodes = (np.cos((np.arange(400) + 0.5) * math.pi / 400) + 1.0) * 0.5 * top
    root = np.sqrt(nodes)
    fits = []
    for values, order in (
        (math.sqrt(2.0) * np.sin(root / 2) / root, 5),
        (math.sqrt(2.0) * np.cos(root / 2), 6),
    ):
        fit = np.polynomial.chebyshev.Chebyshev.fit(nodes, values, order - 1, domain=[0.0, top])
        fits.append([float(v) for v in fit.convert(kind=np.polynomial.Polynomial).coef])
    return fits


SIN_COEF, COS_COEF = half_angle_coefficients()


def weights_kernel(freq_ref, steer_ref, out_ref):
    channel = pl.program_id(1)
    beams = steer_ref.shape[1]
    frequency = freq_ref[channel]
    rows = steer_ref.shape[0]

    def step(index, carry):
        at = pl.ds(pl.multiple_of(index * 16, 16), 16)
        phase = np.float32(2.0 * math.pi) * (frequency * steer_ref[at, :])
        cosine, sines = sincos(phase)
        out_ref[0, at, :beams] = cosine.astype(jnp.bfloat16)
        out_ref[0, at, beams:] = sines.astype(jnp.bfloat16)
        return carry

    lax.fori_loop(0, rows // 16, step, 0)


def beam_weights(frequency, steering_t):
    antennas, beams = steering_t.shape
    channels = frequency.shape[0]
    block = min(512, antennas)
    return pl.pallas_call(
        weights_kernel,
        grid=(antennas // block, channels),
        in_specs=[
            pl.BlockSpec(memory_space=pltpu.SMEM),
            pl.BlockSpec((block, beams), lambda a, c: (a, 0)),
        ],
        out_specs=pl.BlockSpec((1, block, 2 * beams), lambda a, c: (c, a, 0)),
        out_shape=jax.ShapeDtypeStruct((channels, antennas, 2 * beams), jnp.bfloat16),
        compiler_params=pltpu.CompilerParams(vmem_limit_bytes=32 * MIB),
        cost_estimate=pl.CostEstimate(
            flops=30 * channels * antennas * beams,
            bytes_accessed=4 * channels * antennas * beams,
            transcendentals=2 * channels * antennas * beams,
        ),
        name="weights",
    )(frequency, steering_t)


def beam_kernel(wide, tm, first, before_ref, data_ref, weight_ref, power_ref, sum_ref, gather_ref, acc_ref):
    channel = pl.program_id(0)
    groups = data_ref.shape[2]
    antennas = data_ref.shape[4]
    rows = groups * 16
    for w in range(wide):
        for m in range(tm):
            gather_ref[m * rows : (m + 1) * rows, w * antennas : (w + 1) * antennas] = data_ref[
                w * tm + m, 0
            ].reshape(rows, antennas)
    products = jnp.dot(gather_ref[...], weight_ref[0], preferred_element_type=jnp.float32)
    beams = products.shape[1] // 2
    products = products.reshape(tm * groups, 2, 8, 2 * beams)
    real_in = products[:, 0]
    imag_in = products[:, 1]
    beam_real = real_in[..., :beams] + imag_in[..., beams:]
    beam_imag = imag_in[..., :beams] - real_in[..., beams:]
    power = beam_real * beam_real + beam_imag * beam_imag
    power_ref[0] = power.reshape(tm * groups * 8, beams)
    total = jnp.sum(jnp.sum(power, axis=0), axis=(0, 1), keepdims=True)
    lane = lax.broadcasted_iota(jnp.int32, acc_ref.shape, 1)

    @pl.when(channel == 0)
    def _():
        acc_ref[...] = before_ref[:1, :]

    acc_ref[...] = jnp.where(lane == channel + first, total, acc_ref[...])

    @pl.when(channel == pl.num_programs(0) - 1)
    def _():
        sum_ref[...] = jnp.broadcast_to(acc_ref[...], sum_ref.shape)


def form_beams(received, weights, before, first, wide, tm):
    devices, channels, groups, _, antennas = received.shape
    _, antenna_full, twice = weights.shape
    frames = tm * groups * 8
    beams = twice // 2
    return pl.pallas_call(
        functools.partial(beam_kernel, wide, tm, first),
        grid=(channels,),
        in_specs=[
            pl.BlockSpec((devices, 128), lambda c: (0, 0)),
            pl.BlockSpec((devices, 1, groups, 16, antennas), lambda c: (0, c, 0, 0, 0)),
            pl.BlockSpec((1, antenna_full, twice), lambda c: (c + first, 0, 0)),
        ],
        out_specs=[
            pl.BlockSpec((1, frames, beams), lambda c: (c, 0, 0)),
            pl.BlockSpec((devices, 128), lambda c: (0, 0)),
        ],
        out_shape=[
            jax.ShapeDtypeStruct((channels, frames, beams), jnp.float32),
            jax.ShapeDtypeStruct((devices, 128), jnp.float32),
        ],
        scratch_shapes=[
            pltpu.VMEM((2 * frames, antenna_full), jnp.bfloat16),
            pltpu.VMEM((1, 128), jnp.float32),
        ],
        compiler_params=pltpu.CompilerParams(vmem_limit_bytes=48 * MIB),
        cost_estimate=pl.CostEstimate(
            flops=4 * channels * frames * antenna_full * twice,
            bytes_accessed=2 * channels * antenna_full * twice,
            transcendentals=0,
        ),
        name="beams",
    )(before, received, weights)


def level_kernel(wide, tm, mask_ref, count_ref, sums_ref, *refs):
    power_refs, out_ref = refs[:-1], refs[-1]
    channels = mask_ref.shape[0]
    _, frames, beams = power_refs[0].shape
    slots = [(ref, c) for ref in power_refs for c in range(ref.shape[0])]
    own_beams = beams // wide
    own_frames = frames // tm
    per_row = max(1, 128 // own_beams)
    sums = sums_ref[...]
    means = []
    for c in range(channels):
        means.append(jnp.sum(jnp.sum(mask_ref[c] * sums, axis=0, keepdims=True), axis=1, keepdims=True))
    mean = jnp.concatenate(means, axis=0) / count_ref[...]

    def level(f):
        value = jnp.concatenate([ref[c, f : f + 1, :] for ref, c in slots], axis=0)
        return (value / mean).astype(jnp.bfloat16)

    for start in range(0, frames, per_row):
        values = [level(f) for f in range(start, start + per_row)]
        for w in range(wide):
            piece = jnp.concatenate(
                [v[:, w * own_beams : (w + 1) * own_beams] for v in values], axis=1
            )
            m, at = divmod(start, own_frames)
            at *= own_beams
            out_ref[w * tm + m, :, at : at + per_row * own_beams] = piece


def form_levels(mask, count, sums, powers, wide, tm):
    channels = mask.shape[0]
    _, frames, beams = powers[0].shape
    lanes = frames // tm * (beams // wide)
    return pl.pallas_call(
        functools.partial(level_kernel, wide, tm),
        out_shape=jax.ShapeDtypeStruct((wide * tm, channels, lanes), jnp.bfloat16),
        compiler_params=pltpu.CompilerParams(vmem_limit_bytes=48 * MIB),
        name="levels",
    )(mask, count, sums, *powers)


def turn(source_ref, lane, lanes, target_ref, row):
    for start in range(0, lanes, 128):
        size = min(128, lanes - start)
        piece = source_ref[:, lane + start : lane + start + size].T
        target_ref[row + start : row + start + size, :] = piece


def dedisperse(turn_ref, pick_ref, sum_ref, row, frames, beams):
    chunk = 7
    for start in range(0, frames, chunk):
        stop = min(start + chunk, frames)
        held = jnp.concatenate(
            [
                turn_ref[(start + d) * beams : (stop + d) * beams, :]
                for d in range(MAXDELAY + 1)
            ],
            axis=1,
        )
        sum_ref[0, row + start * beams : row + stop * beams, :] = jnp.dot(
            held, pick_ref[...], preferred_element_type=jnp.float32
        )


def boxcars(channels, width_ref, sum_ref, stage_ref, out_ref, sems, row, beams):
    widths, rows, _ = stage_ref.shape
    for at in range(0, rows, 2 * beams):
        total = sum_ref[0, at : at + 2 * beams, :]
        for lag in range(1, WMAX):
            begin = at + lag * beams
            total = total + sum_ref[0, begin : begin + 2 * beams, :]
            sum_ref[lag, at : at + 2 * beams, :] = total
    copies = []
    for i in range(widths):
        expected = width_ref[i].astype(jnp.float32) * np.float32(channels)
        root = jnp.sqrt(jnp.full((1, stage_ref.shape[2]), expected, jnp.float32))
        stage_ref[i] = (sum_ref[width_ref[i] - 1, :rows, :] - expected) / root
        copy = pltpu.make_async_copy(
            stage_ref.at[i], out_ref.at[i, pl.ds(row, rows)], sems.at[i]
        )
        copy.start()
        copies.append(copy)
    for copy in copies:
        copy.wait()


def search_early_kernel(
    beams, width_ref, pick_ref, level_ref, out_ref, kept_ref, turn_ref, sum_ref, stage_ref, sems
):
    channels, lanes = level_ref.shape
    turn(level_ref, 0, lanes, turn_ref, 0)
    known = sum_ref.shape[1]
    dedisperse(turn_ref, pick_ref, sum_ref, 0, known // beams, beams)
    kept_ref[...] = sum_ref[0, known - kept_ref.shape[0] :, :]
    boxcars(channels, width_ref, sum_ref, stage_ref, out_ref, sems, 0, beams)


def search_late_kernel(
    beams, width_ref, pick_ref, level_ref, halo_ref, kept_ref, given_ref, out_ref, turn_ref,
    sum_ref, stage_ref, sems,
):
    channels, lanes = level_ref.shape
    held = MAXDELAY * beams
    turn(level_ref, lanes - held, held, turn_ref, 0)
    turn(halo_ref, 0, halo_ref.shape[1], turn_ref, held)
    kept = kept_ref.shape[0]
    sum_ref[0, :kept, :] = kept_ref[...]
    dedisperse(turn_ref, pick_ref, sum_ref, kept, sum_ref.shape[1] // beams - WMAX + 1, beams)
    row = lanes - stage_ref.shape[1]
    boxcars(channels, width_ref, sum_ref, stage_ref, out_ref, sems, row, beams)


def search(box_widths, picks, levels, beams):
    trials = picks.shape[1]
    channels, lanes = levels.shape
    widths = box_widths.shape[0]
    lags = WMAX - 1
    frames = lanes // beams
    known = frames - MAXDELAY
    early = known - lags
    late = frames - early
    whole = pl.BlockSpec(memory_space=pltpu.VMEM)
    params = pltpu.CompilerParams(vmem_limit_bytes=32 * MIB)
    found, kept = pl.pallas_call(
        functools.partial(search_early_kernel, beams),
        in_specs=[pl.BlockSpec(memory_space=pltpu.SMEM), whole, whole],
        out_specs=[pl.BlockSpec(memory_space=pl.ANY), whole],
        out_shape=[
            jax.ShapeDtypeStruct((widths, lanes, trials), jnp.float32),
            jax.ShapeDtypeStruct((lags * beams, trials), jnp.float32),
        ],
        scratch_shapes=[
            pltpu.VMEM((lanes, channels), jnp.bfloat16),
            pltpu.VMEM((WMAX, known * beams, trials), jnp.float32),
            pltpu.VMEM((widths, early * beams, trials), jnp.float32),
            pltpu.SemaphoreType.DMA((widths,)),
        ],
        compiler_params=params,
        name="search_early",
    )(box_widths, picks, levels)
    blocks = lax.axis_size("tm")
    halo = lax.ppermute(
        levels[:, : (MAXDELAY + lags) * beams], "tm", [(i, (i - 1) % blocks) for i in range(blocks)]
    )
    return pl.pallas_call(
        functools.partial(search_late_kernel, beams),
        in_specs=[
            pl.BlockSpec(memory_space=pltpu.SMEM),
            whole,
            whole,
            whole,
            whole,
            pl.BlockSpec(memory_space=pl.ANY),
        ],
        out_specs=pl.BlockSpec(memory_space=pl.ANY),
        out_shape=jax.ShapeDtypeStruct((widths, lanes, trials), jnp.float32),
        scratch_shapes=[
            pltpu.VMEM(((MAXDELAY + MAXDELAY + lags) * beams, channels), jnp.bfloat16),
            pltpu.VMEM((WMAX, (late + lags) * beams, trials), jnp.float32),
            pltpu.VMEM((widths, late * beams, trials), jnp.float32),
            pltpu.SemaphoreType.DMA((widths,)),
        ],
        input_output_aliases={5: 0},
        compiler_params=params,
        name="search_late",
    )(box_widths, picks, levels, halo, kept, found)


def exchange(value):
    return lax.all_to_all(value, AXES, split_axis=0, concat_axis=0, tiled=True)


def body(voltages, fir_taps, steering, band_widths, delays, box_widths):
    wide = lax.axis_size("wide")
    tm = lax.axis_size("tm")
    devices = wide * tm
    taps, channel_rows = fir_taps.shape
    antenna_local = voltages.shape[1]
    beam_count = steering.shape[0]
    sample_count = voltages.shape[2]
    frame_rows = sample_count // channel_rows
    total_frames = frame_rows * tm
    slots = channel_rows // devices
    own = lax.axis_index("wide") * tm + lax.axis_index("tm")
    own_ids = own * slots + jnp.arange(slots, dtype=jnp.int32)

    lookback = (taps - 1) * channel_rows
    halo = lax.ppermute(
        voltages[:, :, sample_count - lookback :], "tm", [(i, (i + 1) % tm) for i in range(tm)]
    )
    parts = slot_parts(slots)
    counts = [devices * part for part in parts]
    table = pltpu.with_memory_space_constraint(
        jnp.asarray(dft_rows(channel_rows, slots)), pltpu.HBM
    )
    fir_taps = pltpu.with_memory_space_constraint(fir_taps, pltpu.HBM)
    voltages = pltpu.with_memory_space_constraint(voltages, pltpu.HBM)
    early, tail = spectra(counts, table, halo, voltages, fir_taps)
    groups = frame_rows // 8

    def arrive(piece, part):
        received = exchange(piece.reshape(devices, part * groups * 16, antenna_local))
        return received.reshape(devices, part, groups, 16, antenna_local)

    frequency = 1.0 + own_ids.astype(jnp.float32) / channel_rows
    early, frequency, steering = lax.optimization_barrier((early, frequency, steering))
    weights = beam_weights(frequency, steering.T)
    early = arrive(early, parts[0])
    early, tail, weights = lax.optimization_barrier((early, tail, weights))
    sums = jnp.zeros((devices, 128), jnp.float32)
    power, sums = form_beams(early, weights, sums, 0, wide, tm)
    late, sums = form_beams(arrive(tail, parts[1]), weights, sums, parts[0], wide, tm)
    powers = [power, late]

    starts = jnp.cumsum(band_widths) - band_widths
    ids = jnp.arange(channel_rows, dtype=jnp.int32)
    bands = jnp.sum((ids[:, None] >= starts[None, :]).astype(jnp.int32), axis=1) - 1
    own_band = jnp.sum((own_ids[:, None] >= starts[None, :]).astype(jnp.int32), axis=1) - 1
    mask = (own_band[:, None] == bands[None, :]).astype(jnp.float32)
    mask = jnp.pad(mask.reshape(slots, devices, slots), ((0, 0), (0, 0), (0, 128 - slots)))
    count = jnp.sum(
        jnp.where(
            own_band[:, None] == jnp.arange(band_widths.shape[0], dtype=jnp.int32)[None, :],
            band_widths.astype(jnp.float32)[None, :] * (total_frames * beam_count),
            0.0,
        ),
        axis=1,
        keepdims=True,
    )
    levels = form_levels(mask, count, exchange(sums), powers, wide, tm)
    arrived = exchange(levels).reshape(channel_rows, levels.shape[2])

    steps = jnp.arange(MAXDELAY + 1, dtype=jnp.int32)
    picks = (delays.T[None, :, :] == steps[:, None, None]).astype(jnp.bfloat16)
    picks = picks.reshape((MAXDELAY + 1) * channel_rows, delays.shape[0])
    own_beams = beam_count // wide
    found = search(box_widths, picks, arrived, own_beams)
    found = found.reshape(box_widths.shape[0], frame_rows, own_beams, delays.shape[0])
    return found.transpose(3, 0, 1, 2)


def solution(mesh):
    return jax.shard_map(
        body,
        mesh=mesh,
        in_specs=(P(None, "wide", "tm"), P(), P(), P(), P(), P()),
        out_specs=P(None, None, "tm", "wide"),
        check_vma=False,
    )
```

```python
import functools
import math

import jax
import jax.numpy as jnp
import numpy as np
from jax import lax
from jax.experimental import pallas as pl
from jax.experimental.pallas import tpu as pltpu
from jax.sharding import PartitionSpec as P

MAXDELAY = 7
WMAX = 8
AXES = ("wide", "tm")
MIB = 1 << 20


def slot_parts(slots):
    late = max(1, slots // 8)
    return slots - late, late


def dft_rows(channel_rows, slots):
    positions = np.arange(channel_rows, dtype=np.int64)
    product = (positions[:, None] * positions[None, :] % channel_rows).astype(np.float32)
    angles = np.float32(2.0 * math.pi / channel_rows) * product
    cosine = np.cos(angles.astype(np.float64)).astype(np.float32)
    sines = np.sin(angles.astype(np.float64)).astype(np.float32)
    real_rows = np.concatenate([cosine.T, sines.T], axis=1)
    imag_rows = np.concatenate([-sines.T, cosine.T], axis=1)
    rows = np.stack([real_rows, imag_rows], axis=1).reshape(-1, slots, 2, 2 * channel_rows)
    first = 0
    ordered = []
    for count in slot_parts(slots):
        ordered.append(rows[:, first : first + count].reshape(-1, 2 * channel_rows))
        first += count
    return np.concatenate(ordered).astype(jnp.bfloat16)


def transform(inners, skip, taps_ref, table_ref, past_ref, volt_ref, part_ref):
    taps = taps_ref.shape[0]
    width = taps_ref.shape[1]
    for inner in inners:
        pieces = []
        for part in range(2):
            total = None
            for back in range(taps):
                if inner >= back:
                    at = (inner - back) * width
                    value = volt_ref[part, :, at : at + width]
                else:
                    at = skip + (taps - 1 + inner - back) * width
                    value = past_ref[part, :, at : at + width]
                term = taps_ref[back : back + 1, :] * value.astype(jnp.float32)
                total = term if total is None else total + term
            pieces.append(total.astype(jnp.bfloat16))
        filtered = jnp.concatenate(pieces, axis=1)
        spectrum = lax.dot_general(
            table_ref[...], filtered, (((1,), (1,)), ((), ())), preferred_element_type=jnp.float32
        )
        rows, antennas = spectrum.shape
        lanes = part_ref.shape[0] * 128
        if lanes > antennas:
            spectrum = jnp.concatenate(
                [spectrum, jnp.zeros((rows, lanes - antennas), jnp.float32)], axis=1
            )
        for half in range(lanes // 128):
            part_ref[half, pl.ds(inner, rows, stride=8), :] = spectrum[
                :, half * 128 : half * 128 + 128
            ]


def write_out(part_ref, out_refs, kept_ref=None, fresh=8):
    antennas = out_refs[0].shape[3]
    for half in range(part_ref.shape[0]):
        size = min(128, antennas - half * 128)
        first = 0
        for out_ref in out_refs:
            count = out_ref.shape[0]
            value = part_ref[half, first * 16 : (first + count) * 16]
            if kept_ref is not None:
                kept = kept_ref[half, first * 16 : (first + count) * 16]
                frame = lax.broadcasted_iota(jnp.int32, value.shape, 0) % 8
                value = jnp.where(frame < fresh, value, kept)
            value = value.astype(jnp.bfloat16).reshape(count, 16, 128)
            out_ref[:, 0, :, half * 128 : half * 128 + size] = value[:, :, :size]
            first += count


def spectra_kernel(skip, taps_ref, table_ref, past_ref, volt_ref, *rest):
    out_refs, kept_ref, part_ref = rest[:-2], rest[-2], rest[-1]
    taps = taps_ref.shape[0]

    @pl.when(pl.program_id(0) == 0)
    def _():
        transform(range(taps - 1, 8), 0, taps_ref, table_ref, past_ref, volt_ref, kept_ref)

    @pl.when(pl.program_id(0) > 0)
    def _():
        transform(range(8), skip, taps_ref, table_ref, past_ref, volt_ref, part_ref)
        write_out(part_ref, out_refs)


def spectra_first_kernel(taps_ref, table_ref, past_ref, volt_ref, kept_ref, *rest):
    count = (len(rest) - 1) // 2
    out_refs, part_ref = rest[count:-1], rest[-1]
    fresh = taps_ref.shape[0] - 1
    transform(range(fresh), 0, taps_ref, table_ref, past_ref, volt_ref, part_ref)
    write_out(part_ref, out_refs, kept_ref.at[pl.ds(pl.program_id(0), 1)], fresh)


def spectra(counts, table, halo, voltages, fir_taps):
    taps, width = fir_taps.shape
    antennas = voltages.shape[1]
    groups = voltages.shape[2] // (8 * width)
    part = pltpu.VMEM((-(-antennas // 128), 2 * width * 8, 128), jnp.float32)
    shapes = [pltpu.HBM((count, groups, 16, antennas), jnp.bfloat16) for count in counts]

    size = 128 if antennas % 128 == 0 else antennas

    def blocks(place, size):
        return [pl.BlockSpec((count, 1, 16, size), place) for count in counts]

    def cost(frames):
        return pl.CostEstimate(
            flops=8 * frames * antennas * width * width,
            bytes_accessed=8 * frames * antennas * width,
            transcendentals=0,
        )

    common = [
        pl.BlockSpec(fir_taps.shape, lambda g: (0, 0)),
        pl.BlockSpec(table.shape, lambda g: (0, 0)),
    ]
    *outgoing, kept = pl.pallas_call(
        functools.partial(spectra_kernel, (5 - taps) * width),
        grid=(groups,),
        in_specs=common
        + [
            pl.BlockSpec((2, antennas, 4 * width), lambda g: (0, 0, jnp.maximum(2 * g - 1, 1))),
            pl.BlockSpec((2, antennas, 8 * width), lambda g: (0, 0, g)),
        ],
        out_specs=blocks(lambda g: (0, jnp.maximum(g, 1), 0, 0), antennas)
        + [pl.BlockSpec(memory_space=pltpu.VMEM)],
        out_shape=shapes + [part],
        scratch_shapes=[part],
        compiler_params=pltpu.CompilerParams(vmem_limit_bytes=40 * MIB),
        cost_estimate=cost(8 * groups),
        name="spectra",
    )(fir_taps, table, voltages, voltages)
    kept = pltpu.with_memory_space_constraint(kept, pltpu.VMEM)
    return pl.pallas_call(
        spectra_first_kernel,
        grid=(antennas // size,),
        in_specs=common
        + [
            pl.BlockSpec((2, size, halo.shape[2]), lambda h: (0, h, 0)),
            pl.BlockSpec((2, size, 4 * width), lambda h: (0, h, 0)),
            pl.BlockSpec(memory_space=pltpu.VMEM),
        ]
        + [pl.BlockSpec(memory_space=pl.ANY)] * len(counts),
        out_specs=blocks(lambda h: (0, 0, 0, h), size),
        out_shape=shapes,
        scratch_shapes=[pltpu.VMEM((1, 2 * width * 8, 128), jnp.float32)],
        input_output_aliases={5 + i: i for i in range(len(counts))},
        compiler_params=pltpu.CompilerParams(vmem_limit_bytes=32 * MIB),
        cost_estimate=cost(taps - 1),
        name="spectra_first",
    )(fir_taps, table, halo, voltages, kept, *outgoing)


def sincos(phase):
    turns = jnp.round(phase * np.float32(1.0 / (2.0 * math.pi)))
    high = np.float32(6.28125)
    middle = np.float32(np.round((2.0 * math.pi - 6.28125) * 2.0**26) / 2.0**26)
    low = np.float32(2.0 * math.pi - 6.28125 - float(middle))
    rest = phase - turns * high
    rest = rest - turns * middle
    rest = rest - turns * low
    square = rest * rest
    s = np.float32(SIN_COEF[-1])
    for value in SIN_COEF[-2::-1]:
        s = s * square + np.float32(value)
    s = s * rest
    c = np.float32(COS_COEF[-1])
    for value in COS_COEF[-2::-1]:
        c = c * square + np.float32(value)
    return np.float32(1.0) - s * s, s * c


def half_angle_coefficients():
    top = (math.pi + 0.01) ** 2
    nodes = (np.cos((np.arange(400) + 0.5) * math.pi / 400) + 1.0) * 0.5 * top
    root = np.sqrt(nodes)
    fits = []
    for values, order in (
        (math.sqrt(2.0) * np.sin(root / 2) / root, 5),
        (math.sqrt(2.0) * np.cos(root / 2), 6),
    ):
        fit = np.polynomial.chebyshev.Chebyshev.fit(nodes, values, order - 1, domain=[0.0, top])
        fits.append([float(v) for v in fit.convert(kind=np.polynomial.Polynomial).coef])
    return fits


SIN_COEF, COS_COEF = half_angle_coefficients()


def weights_kernel(freq_ref, steer_ref, out_ref):
    channel = pl.program_id(1)
    beams = steer_ref.shape[1]
    frequency = freq_ref[channel]
    rows = steer_ref.shape[0]

    def step(index, carry):
        at = pl.ds(pl.multiple_of(index * 16, 16), 16)
        phase = np.float32(2.0 * math.pi) * (frequency * steer_ref[at, :])
        cosine, sines = sincos(phase)
        out_ref[0, at, :beams] = cosine.astype(jnp.bfloat16)
        out_ref[0, at, beams:] = sines.astype(jnp.bfloat16)
        return carry

    lax.fori_loop(0, rows // 16, step, 0)


def beam_weights(frequency, steering_t):
    antennas, beams = steering_t.shape
    channels = frequency.shape[0]
    block = min(512, antennas)
    return pl.pallas_call(
        weights_kernel,
        grid=(antennas // block, channels),
        in_specs=[
            pl.BlockSpec(memory_space=pltpu.SMEM),
            pl.BlockSpec((block, beams), lambda a, c: (a, 0)),
        ],
        out_specs=pl.BlockSpec((1, block, 2 * beams), lambda a, c: (c, a, 0)),
        out_shape=jax.ShapeDtypeStruct((channels, antennas, 2 * beams), jnp.bfloat16),
        compiler_params=pltpu.CompilerParams(vmem_limit_bytes=32 * MIB),
        cost_estimate=pl.CostEstimate(
            flops=30 * channels * antennas * beams,
            bytes_accessed=4 * channels * antennas * beams,
            transcendentals=2 * channels * antennas * beams,
        ),
        name="weights",
    )(frequency, steering_t)


def beam_kernel(
    wide, tm, first, before_ref, data_ref, weight_ref, power_ref, sum_ref, gather_ref, acc_ref,
    *rest,
):
    channel = pl.program_id(0)
    copies = []
    if rest:
        held_ref, sems = rest
        steps = sems.shape[0]
        depth = held_ref.shape[0] // steps
        for step in range(steps):
            rows = pl.ds(step * depth, depth)
            copies.append(
                pltpu.make_async_copy(
                    weight_ref.at[channel + first, rows], held_ref.at[rows], sems.at[step]
                )
            )
            copies[-1].start()
    groups = data_ref.shape[2]
    antennas = data_ref.shape[4]
    rows = groups * 16
    for w in range(wide):
        for m in range(tm):
            gather_ref[m * rows : (m + 1) * rows, w * antennas : (w + 1) * antennas] = data_ref[
                w * tm + m, 0
            ].reshape(rows, antennas)
    if copies:
        products = None
        for step, copy in enumerate(copies):
            copy.wait()
            own = slice(step * depth, (step + 1) * depth)
            term = jnp.dot(
                gather_ref[:, own], held_ref[own, :], preferred_element_type=jnp.float32
            )
            products = term if products is None else products + term
    else:
        products = jnp.dot(gather_ref[...], weight_ref[0], preferred_element_type=jnp.float32)
    beams = products.shape[1] // 2
    products = products.reshape(tm * groups, 2, 8, 2 * beams)
    real_in = products[:, 0]
    imag_in = products[:, 1]
    beam_real = real_in[..., :beams] + imag_in[..., beams:]
    beam_imag = imag_in[..., :beams] - real_in[..., beams:]
    power = beam_real * beam_real + beam_imag * beam_imag
    power_ref[0] = power.reshape(tm * groups * 8, beams)
    total = jnp.sum(jnp.sum(power, axis=0), axis=(0, 1), keepdims=True)
    lane = lax.broadcasted_iota(jnp.int32, acc_ref.shape, 1)

    @pl.when(channel == 0)
    def _():
        acc_ref[...] = before_ref[:1, :]

    acc_ref[...] = jnp.where(lane == channel + first, total, acc_ref[...])

    @pl.when(channel == pl.num_programs(0) - 1)
    def _():
        sum_ref[...] = jnp.broadcast_to(acc_ref[...], sum_ref.shape)


def form_beams(received, weights, before, first, wide, tm, quarters):
    devices, channels, groups, _, antennas = received.shape
    _, antenna_full, twice = weights.shape
    frames = tm * groups * 8
    beams = twice // 2
    return pl.pallas_call(
        functools.partial(beam_kernel, wide, tm, first),
        grid=(channels,),
        in_specs=[
            pl.BlockSpec((devices, 128), lambda c: (0, 0)),
            pl.BlockSpec((devices, 1, groups, 16, antennas), lambda c: (0, c, 0, 0, 0)),
            pl.BlockSpec(memory_space=pl.ANY)
            if quarters
            else pl.BlockSpec((1, antenna_full, twice), lambda c: (c + first, 0, 0)),
        ],
        out_specs=[
            pl.BlockSpec((1, frames, beams), lambda c: (c, 0, 0)),
            pl.BlockSpec((devices, 128), lambda c: (0, 0)),
        ],
        out_shape=[
            jax.ShapeDtypeStruct((channels, frames, beams), jnp.float32),
            jax.ShapeDtypeStruct((devices, 128), jnp.float32),
        ],
        scratch_shapes=[
            pltpu.VMEM((2 * frames, antenna_full), jnp.bfloat16),
            pltpu.VMEM((1, 128), jnp.float32),
        ]
        + (
            [
                pltpu.VMEM((antenna_full, twice), jnp.bfloat16),
                pltpu.SemaphoreType.DMA((quarters,)),
            ]
            if quarters
            else []
        ),
        compiler_params=pltpu.CompilerParams(vmem_limit_bytes=48 * MIB),
        cost_estimate=pl.CostEstimate(
            flops=4 * channels * frames * antenna_full * twice,
            bytes_accessed=2 * channels * antenna_full * twice,
            transcendentals=0,
        ),
        name="beams",
    )(before, received, weights)


def level_kernel(wide, tm, mask_ref, count_ref, sums_ref, *refs):
    power_refs, out_ref = refs[:-1], refs[-1]
    channels = mask_ref.shape[0]
    _, frames, beams = power_refs[0].shape
    slots = [(ref, c) for ref in power_refs for c in range(ref.shape[0])]
    own_beams = beams // wide
    own_frames = frames // tm
    per_row = max(1, 128 // own_beams)
    sums = sums_ref[...]
    means = []
    for c in range(channels):
        means.append(jnp.sum(jnp.sum(mask_ref[c] * sums, axis=0, keepdims=True), axis=1, keepdims=True))
    mean = jnp.concatenate(means, axis=0) / count_ref[...]

    def level(f):
        value = jnp.concatenate([ref[c, f : f + 1, :] for ref, c in slots], axis=0)
        return (value / mean).astype(jnp.bfloat16)

    for start in range(0, frames, per_row):
        values = [level(f) for f in range(start, start + per_row)]
        for w in range(wide):
            piece = jnp.concatenate(
                [v[:, w * own_beams : (w + 1) * own_beams] for v in values], axis=1
            )
            m, at = divmod(start, own_frames)
            at *= own_beams
            out_ref[w * tm + m, :, at : at + per_row * own_beams] = piece


def form_levels(mask, count, sums, powers, wide, tm):
    channels = mask.shape[0]
    _, frames, beams = powers[0].shape
    lanes = frames // tm * (beams // wide)
    return pl.pallas_call(
        functools.partial(level_kernel, wide, tm),
        out_shape=jax.ShapeDtypeStruct((wide * tm, channels, lanes), jnp.bfloat16),
        compiler_params=pltpu.CompilerParams(vmem_limit_bytes=48 * MIB),
        name="levels",
    )(mask, count, sums, *powers)


def turn(source_ref, lane, lanes, target_ref, row):
    for start in range(0, lanes, 128):
        size = min(128, lanes - start)
        piece = source_ref[:, lane + start : lane + start + size].T
        target_ref[row + start : row + start + size, :] = piece


def dedisperse(turn_ref, pick_ref, sum_ref, row, frames, beams):
    chunk = 7
    for start in range(0, frames, chunk):
        stop = min(start + chunk, frames)
        held = jnp.concatenate(
            [
                turn_ref[(start + d) * beams : (stop + d) * beams, :]
                for d in range(MAXDELAY + 1)
            ],
            axis=1,
        )
        sum_ref[0, row + start * beams : row + stop * beams, :] = jnp.dot(
            held, pick_ref[...], preferred_element_type=jnp.float32
        )


def boxcars(channels, width_ref, sum_ref, stage_ref, out_ref, sems, row, beams):
    widths, rows, _ = stage_ref.shape
    for at in range(0, rows, 2 * beams):
        total = sum_ref[0, at : at + 2 * beams, :]
        for lag in range(1, WMAX):
            begin = at + lag * beams
            total = total + sum_ref[0, begin : begin + 2 * beams, :]
            sum_ref[lag, at : at + 2 * beams, :] = total
    copies = []
    for i in range(widths):
        expected = width_ref[i].astype(jnp.float32) * np.float32(channels)
        root = jnp.sqrt(jnp.full((1, stage_ref.shape[2]), expected, jnp.float32))
        stage_ref[i] = (sum_ref[width_ref[i] - 1, :rows, :] - expected) / root
        copy = pltpu.make_async_copy(
            stage_ref.at[i], out_ref.at[i, pl.ds(row, rows)], sems.at[i]
        )
        copy.start()
        copies.append(copy)
    for copy in copies:
        copy.wait()


def search_early_kernel(
    beams, width_ref, pick_ref, level_ref, out_ref, kept_ref, turn_ref, sum_ref, stage_ref, sems
):
    channels, lanes = level_ref.shape
    turn(level_ref, 0, lanes, turn_ref, 0)
    known = sum_ref.shape[1]
    dedisperse(turn_ref, pick_ref, sum_ref, 0, known // beams, beams)
    kept_ref[...] = sum_ref[0, known - kept_ref.shape[0] :, :]
    boxcars(channels, width_ref, sum_ref, stage_ref, out_ref, sems, 0, beams)


def search_late_kernel(
    beams, width_ref, pick_ref, level_ref, halo_ref, kept_ref, given_ref, out_ref, turn_ref,
    sum_ref, stage_ref, sems,
):
    channels, lanes = level_ref.shape
    held = MAXDELAY * beams
    turn(level_ref, lanes - held, held, turn_ref, 0)
    turn(halo_ref, 0, halo_ref.shape[1], turn_ref, held)
    kept = kept_ref.shape[0]
    sum_ref[0, :kept, :] = kept_ref[...]
    dedisperse(turn_ref, pick_ref, sum_ref, kept, sum_ref.shape[1] // beams - WMAX + 1, beams)
    row = lanes - stage_ref.shape[1]
    boxcars(channels, width_ref, sum_ref, stage_ref, out_ref, sems, row, beams)


def search(box_widths, picks, levels, beams):
    trials = picks.shape[1]
    channels, lanes = levels.shape
    widths = box_widths.shape[0]
    lags = WMAX - 1
    frames = lanes // beams
    known = frames - MAXDELAY
    early = known - lags
    late = frames - early
    whole = pl.BlockSpec(memory_space=pltpu.VMEM)
    params = pltpu.CompilerParams(vmem_limit_bytes=32 * MIB)
    found, kept = pl.pallas_call(
        functools.partial(search_early_kernel, beams),
        in_specs=[pl.BlockSpec(memory_space=pltpu.SMEM), whole, whole],
        out_specs=[pl.BlockSpec(memory_space=pl.ANY), whole],
        out_shape=[
            jax.ShapeDtypeStruct((widths, lanes, trials), jnp.float32),
            jax.ShapeDtypeStruct((lags * beams, trials), jnp.float32),
        ],
        scratch_shapes=[
            pltpu.VMEM((lanes, channels), jnp.bfloat16),
            pltpu.VMEM((WMAX, known * beams, trials), jnp.float32),
            pltpu.VMEM((widths, early * beams, trials), jnp.float32),
            pltpu.SemaphoreType.DMA((widths,)),
        ],
        compiler_params=params,
        name="search_early",
    )(box_widths, picks, levels)
    blocks = lax.axis_size("tm")
    halo = lax.ppermute(
        levels[:, : (MAXDELAY + lags) * beams], "tm", [(i, (i - 1) % blocks) for i in range(blocks)]
    )
    return pl.pallas_call(
        functools.partial(search_late_kernel, beams),
        in_specs=[
            pl.BlockSpec(memory_space=pltpu.SMEM),
            whole,
            whole,
            whole,
            whole,
            pl.BlockSpec(memory_space=pl.ANY),
        ],
        out_specs=pl.BlockSpec(memory_space=pl.ANY),
        out_shape=jax.ShapeDtypeStruct((widths, lanes, trials), jnp.float32),
        scratch_shapes=[
            pltpu.VMEM(((MAXDELAY + MAXDELAY + lags) * beams, channels), jnp.bfloat16),
            pltpu.VMEM((WMAX, (late + lags) * beams, trials), jnp.float32),
            pltpu.VMEM((widths, late * beams, trials), jnp.float32),
            pltpu.SemaphoreType.DMA((widths,)),
        ],
        input_output_aliases={5: 0},
        compiler_params=params,
        name="search_late",
    )(box_widths, picks, levels, halo, kept, found)


def exchange(value):
    return lax.all_to_all(value, AXES, split_axis=0, concat_axis=0, tiled=True)


def body(voltages, fir_taps, steering, band_widths, delays, box_widths):
    wide = lax.axis_size("wide")
    tm = lax.axis_size("tm")
    devices = wide * tm
    taps, channel_rows = fir_taps.shape
    antenna_local = voltages.shape[1]
    beam_count = steering.shape[0]
    sample_count = voltages.shape[2]
    frame_rows = sample_count // channel_rows
    total_frames = frame_rows * tm
    slots = channel_rows // devices
    own = lax.axis_index("wide") * tm + lax.axis_index("tm")
    own_ids = own * slots + jnp.arange(slots, dtype=jnp.int32)

    lookback = (taps - 1) * channel_rows
    halo = lax.ppermute(
        voltages[:, :, sample_count - lookback :], "tm", [(i, (i + 1) % tm) for i in range(tm)]
    )
    parts = slot_parts(slots)
    counts = [devices * part for part in parts]
    table = pltpu.with_memory_space_constraint(
        jnp.asarray(dft_rows(channel_rows, slots)), pltpu.HBM
    )
    fir_taps = pltpu.with_memory_space_constraint(fir_taps, pltpu.HBM)
    voltages = pltpu.with_memory_space_constraint(voltages, pltpu.HBM)
    early, tail = spectra(counts, table, halo, voltages, fir_taps)
    groups = frame_rows // 8

    def arrive(piece, part):
        received = exchange(piece.reshape(devices, part * groups * 16, antenna_local))
        return received.reshape(devices, part, groups, 16, antenna_local)

    frequency = 1.0 + own_ids.astype(jnp.float32) / channel_rows
    early, frequency, steering = lax.optimization_barrier((early, frequency, steering))
    weights = beam_weights(frequency, steering.T)
    early = arrive(early, parts[0])
    early, tail, weights = lax.optimization_barrier((early, tail, weights))
    sums = jnp.zeros((devices, 128), jnp.float32)
    power, sums = form_beams(early, weights, sums, 0, wide, tm, 0)
    late, sums = form_beams(
        arrive(tail, parts[1]), weights, sums, parts[0], wide, tm, 4
    )
    powers = [power, late]

    starts = jnp.cumsum(band_widths) - band_widths
    ids = jnp.arange(channel_rows, dtype=jnp.int32)
    bands = jnp.sum((ids[:, None] >= starts[None, :]).astype(jnp.int32), axis=1) - 1
    own_band = jnp.sum((own_ids[:, None] >= starts[None, :]).astype(jnp.int32), axis=1) - 1
    mask = (own_band[:, None] == bands[None, :]).astype(jnp.float32)
    mask = jnp.pad(mask.reshape(slots, devices, slots), ((0, 0), (0, 0), (0, 128 - slots)))
    count = jnp.sum(
        jnp.where(
            own_band[:, None] == jnp.arange(band_widths.shape[0], dtype=jnp.int32)[None, :],
            band_widths.astype(jnp.float32)[None, :] * (total_frames * beam_count),
            0.0,
        ),
        axis=1,
        keepdims=True,
    )
    levels = form_levels(mask, count, exchange(sums), powers, wide, tm)
    arrived = exchange(levels).reshape(channel_rows, levels.shape[2])

    steps = jnp.arange(MAXDELAY + 1, dtype=jnp.int32)
    picks = (delays.T[None, :, :] == steps[:, None, None]).astype(jnp.bfloat16)
    picks = picks.reshape((MAXDELAY + 1) * channel_rows, delays.shape[0])
    own_beams = beam_count // wide
    found = search(box_widths, picks, arrived, own_beams)
    found = found.reshape(box_widths.shape[0], frame_rows, own_beams, delays.shape[0])
    return found.transpose(3, 0, 1, 2)


def solution(mesh):
    return jax.shard_map(
        body,
        mesh=mesh,
        in_specs=(P(None, "wide", "tm"), P(), P(), P(), P(), P()),
        out_specs=P(None, None, "tm", "wide"),
        check_vma=False,
    )
```

```python
import functools
import math

import jax
import jax.numpy as jnp
import numpy as np
from jax import lax
from jax.experimental import pallas as pl
from jax.experimental.pallas import tpu as pltpu
from jax.sharding import PartitionSpec as P

MAXDELAY = 7
WMAX = 8
AXES = ("wide", "tm")
MIB = 1 << 20


def slot_parts(slots):
    late = max(1, slots // 8)
    return slots - late, late


def dft_rows(channel_rows, slots):
    positions = np.arange(channel_rows, dtype=np.int64)
    product = (positions[:, None] * positions[None, :] % channel_rows).astype(np.float32)
    angles = np.float32(2.0 * math.pi / channel_rows) * product
    cosine = np.cos(angles.astype(np.float64)).astype(np.float32)
    sines = np.sin(angles.astype(np.float64)).astype(np.float32)
    real_rows = np.concatenate([cosine.T, sines.T], axis=1)
    imag_rows = np.concatenate([-sines.T, cosine.T], axis=1)
    rows = np.stack([real_rows, imag_rows], axis=1).reshape(-1, slots, 2, 2 * channel_rows)
    first = 0
    ordered = []
    for count in slot_parts(slots):
        ordered.append(rows[:, first : first + count].reshape(-1, 2 * channel_rows))
        first += count
    return np.concatenate(ordered).astype(jnp.bfloat16)


def transform(inners, skip, taps_ref, table_ref, past_ref, volt_ref, part_ref):
    taps = taps_ref.shape[0]
    width = taps_ref.shape[1]
    for inner in inners:
        pieces = []
        for part in range(2):
            total = None
            for back in range(taps):
                if inner >= back:
                    at = (inner - back) * width
                    value = volt_ref[part, :, at : at + width]
                else:
                    at = skip + (taps - 1 + inner - back) * width
                    value = past_ref[part, :, at : at + width]
                term = taps_ref[back : back + 1, :] * value.astype(jnp.float32)
                total = term if total is None else total + term
            pieces.append(total.astype(jnp.bfloat16))
        filtered = jnp.concatenate(pieces, axis=1)
        spectrum = lax.dot_general(
            table_ref[...], filtered, (((1,), (1,)), ((), ())), preferred_element_type=jnp.float32
        )
        rows, antennas = spectrum.shape
        lanes = part_ref.shape[0] * 128
        if lanes > antennas:
            spectrum = jnp.concatenate(
                [spectrum, jnp.zeros((rows, lanes - antennas), jnp.float32)], axis=1
            )
        for half in range(lanes // 128):
            part_ref[half, pl.ds(inner, rows, stride=8), :] = spectrum[
                :, half * 128 : half * 128 + 128
            ]


def write_out(part_ref, out_refs, kept_ref=None, fresh=8):
    antennas = out_refs[0].shape[3]
    for half in range(part_ref.shape[0]):
        size = min(128, antennas - half * 128)
        first = 0
        for out_ref in out_refs:
            count = out_ref.shape[0]
            value = part_ref[half, first * 16 : (first + count) * 16]
            if kept_ref is not None:
                kept = kept_ref[half, first * 16 : (first + count) * 16]
                frame = lax.broadcasted_iota(jnp.int32, value.shape, 0) % 8
                value = jnp.where(frame < fresh, value, kept)
            value = value.astype(jnp.bfloat16).reshape(count, 16, 128)
            out_ref[:, 0, :, half * 128 : half * 128 + size] = value[:, :, :size]
            first += count


def spectra_kernel(skip, taps_ref, table_ref, past_ref, volt_ref, *rest):
    out_refs, kept_ref, part_ref = rest[:-2], rest[-2], rest[-1]
    taps = taps_ref.shape[0]

    @pl.when(pl.program_id(0) == 0)
    def _():
        transform(range(taps - 1, 8), 0, taps_ref, table_ref, past_ref, volt_ref, kept_ref)

    @pl.when(pl.program_id(0) > 0)
    def _():
        transform(range(8), skip, taps_ref, table_ref, past_ref, volt_ref, part_ref)
        write_out(part_ref, out_refs)


def spectra_first_kernel(taps_ref, table_ref, past_ref, volt_ref, kept_ref, *rest):
    count = (len(rest) - 1) // 2
    out_refs, part_ref = rest[count:-1], rest[-1]
    fresh = taps_ref.shape[0] - 1
    transform(range(fresh), 0, taps_ref, table_ref, past_ref, volt_ref, part_ref)
    write_out(part_ref, out_refs, kept_ref.at[pl.ds(pl.program_id(0), 1)], fresh)


def spectra(counts, table, halo, voltages, fir_taps):
    taps, width = fir_taps.shape
    antennas = voltages.shape[1]
    groups = voltages.shape[2] // (8 * width)
    part = pltpu.VMEM((-(-antennas // 128), 2 * width * 8, 128), jnp.float32)
    shapes = [pltpu.HBM((count, groups, 16, antennas), jnp.bfloat16) for count in counts]

    size = 128 if antennas % 128 == 0 else antennas

    def blocks(place, size):
        return [pl.BlockSpec((count, 1, 16, size), place) for count in counts]

    def cost(frames):
        return pl.CostEstimate(
            flops=8 * frames * antennas * width * width,
            bytes_accessed=8 * frames * antennas * width,
            transcendentals=0,
        )

    common = [
        pl.BlockSpec(fir_taps.shape, lambda g: (0, 0)),
        pl.BlockSpec(table.shape, lambda g: (0, 0)),
    ]
    *outgoing, kept = pl.pallas_call(
        functools.partial(spectra_kernel, (5 - taps) * width),
        grid=(groups,),
        in_specs=common
        + [
            pl.BlockSpec((2, antennas, 4 * width), lambda g: (0, 0, jnp.maximum(2 * g - 1, 1))),
            pl.BlockSpec((2, antennas, 8 * width), lambda g: (0, 0, g)),
        ],
        out_specs=blocks(lambda g: (0, jnp.maximum(g, 1), 0, 0), antennas)
        + [pl.BlockSpec(memory_space=pltpu.VMEM)],
        out_shape=shapes + [part],
        scratch_shapes=[part],
        compiler_params=pltpu.CompilerParams(vmem_limit_bytes=40 * MIB),
        cost_estimate=cost(8 * groups),
        name="spectra",
    )(fir_taps, table, voltages, voltages)
    kept = pltpu.with_memory_space_constraint(kept, pltpu.VMEM)
    return pl.pallas_call(
        spectra_first_kernel,
        grid=(antennas // size,),
        in_specs=common
        + [
            pl.BlockSpec((2, size, halo.shape[2]), lambda h: (0, h, 0)),
            pl.BlockSpec((2, size, 4 * width), lambda h: (0, h, 0)),
            pl.BlockSpec(memory_space=pltpu.VMEM),
        ]
        + [pl.BlockSpec(memory_space=pl.ANY)] * len(counts),
        out_specs=blocks(lambda h: (0, 0, 0, h), size),
        out_shape=shapes,
        scratch_shapes=[pltpu.VMEM((1, 2 * width * 8, 128), jnp.float32)],
        input_output_aliases={5 + i: i for i in range(len(counts))},
        compiler_params=pltpu.CompilerParams(vmem_limit_bytes=32 * MIB),
        cost_estimate=cost(taps - 1),
        name="spectra_first",
    )(fir_taps, table, halo, voltages, kept, *outgoing)


def sincos(phase):
    turns = jnp.round(phase * np.float32(1.0 / (2.0 * math.pi)))
    high = np.float32(6.28125)
    middle = np.float32(np.round((2.0 * math.pi - 6.28125) * 2.0**26) / 2.0**26)
    low = np.float32(2.0 * math.pi - 6.28125 - float(middle))
    rest = phase - turns * high
    rest = rest - turns * middle
    rest = rest - turns * low
    square = rest * rest
    s = np.float32(SIN_COEF[-1])
    for value in SIN_COEF[-2::-1]:
        s = s * square + np.float32(value)
    s = s * rest
    c = np.float32(COS_COEF[-1])
    for value in COS_COEF[-2::-1]:
        c = c * square + np.float32(value)
    return np.float32(1.0) - s * s, s * c


def half_angle_coefficients():
    top = (math.pi + 0.01) ** 2
    nodes = (np.cos((np.arange(400) + 0.5) * math.pi / 400) + 1.0) * 0.5 * top
    root = np.sqrt(nodes)
    fits = []
    for values, order in (
        (math.sqrt(2.0) * np.sin(root / 2) / root, 5),
        (math.sqrt(2.0) * np.cos(root / 2), 6),
    ):
        fit = np.polynomial.chebyshev.Chebyshev.fit(nodes, values, order - 1, domain=[0.0, top])
        fits.append([float(v) for v in fit.convert(kind=np.polynomial.Polynomial).coef])
    return fits


SIN_COEF, COS_COEF = half_angle_coefficients()


def weights_kernel(freq_ref, steer_ref, out_ref):
    channel = pl.program_id(1)
    beams = steer_ref.shape[1]
    frequency = freq_ref[channel]
    rows = steer_ref.shape[0]

    def step(index, carry):
        at = pl.ds(pl.multiple_of(index * 16, 16), 16)
        phase = np.float32(2.0 * math.pi) * (frequency * steer_ref[at, :])
        cosine, sines = sincos(phase)
        out_ref[0, at, :beams] = cosine.astype(jnp.bfloat16)
        out_ref[0, at, beams:] = sines.astype(jnp.bfloat16)
        return carry

    lax.fori_loop(0, rows // 16, step, 0)


def beam_weights(frequency, steering_t):
    antennas, beams = steering_t.shape
    channels = frequency.shape[0]
    block = min(512, antennas)
    return pl.pallas_call(
        weights_kernel,
        grid=(antennas // block, channels),
        in_specs=[
            pl.BlockSpec(memory_space=pltpu.SMEM),
            pl.BlockSpec((block, beams), lambda a, c: (a, 0)),
        ],
        out_specs=pl.BlockSpec((1, block, 2 * beams), lambda a, c: (c, a, 0)),
        out_shape=jax.ShapeDtypeStruct((channels, antennas, 2 * beams), jnp.bfloat16),
        compiler_params=pltpu.CompilerParams(vmem_limit_bytes=32 * MIB),
        cost_estimate=pl.CostEstimate(
            flops=30 * channels * antennas * beams,
            bytes_accessed=4 * channels * antennas * beams,
            transcendentals=2 * channels * antennas * beams,
        ),
        name="weights",
    )(frequency, steering_t)


def beam_kernel(
    wide, tm, first, before_ref, data_ref, weight_ref, power_ref, sum_ref, gather_ref, acc_ref,
    *rest,
):
    channel = pl.program_id(0)
    copies = []
    if rest:
        held_ref, sems = rest
        steps = sems.shape[0]
        depth = held_ref.shape[0] // steps
        for step in range(steps):
            rows = pl.ds(step * depth, depth)
            copies.append(
                pltpu.make_async_copy(
                    weight_ref.at[channel + first, rows], held_ref.at[rows], sems.at[step]
                )
            )
            copies[-1].start()
    groups = data_ref.shape[2]
    antennas = data_ref.shape[4]
    rows = groups * 16
    for w in range(wide):
        for m in range(tm):
            gather_ref[m * rows : (m + 1) * rows, w * antennas : (w + 1) * antennas] = data_ref[
                w * tm + m, 0
            ].reshape(rows, antennas)
    if copies:
        products = None
        for step, copy in enumerate(copies):
            copy.wait()
            own = slice(step * depth, (step + 1) * depth)
            term = jnp.dot(
                gather_ref[:, own], held_ref[own, :], preferred_element_type=jnp.float32
            )
            products = term if products is None else products + term
    else:
        products = jnp.dot(gather_ref[...], weight_ref[0], preferred_element_type=jnp.float32)
    beams = products.shape[1] // 2
    products = products.reshape(tm * groups, 2, 8, 2 * beams)
    real_in = products[:, 0]
    imag_in = products[:, 1]
    beam_real = real_in[..., :beams] + imag_in[..., beams:]
    beam_imag = imag_in[..., :beams] - real_in[..., beams:]
    power = beam_real * beam_real + beam_imag * beam_imag
    power_ref[0] = power.reshape(tm * groups * 8, beams)
    total = jnp.sum(jnp.sum(power, axis=0), axis=(0, 1), keepdims=True)
    lane = lax.broadcasted_iota(jnp.int32, acc_ref.shape, 1)

    @pl.when(channel == 0)
    def _():
        acc_ref[...] = before_ref[:1, :]

    acc_ref[...] = jnp.where(lane == channel + first, total, acc_ref[...])

    @pl.when(channel == pl.num_programs(0) - 1)
    def _():
        sum_ref[...] = jnp.broadcast_to(acc_ref[...], sum_ref.shape)


def form_beams(received, weights, before, first, wide, tm, quarters):
    devices, channels, groups, _, antennas = received.shape
    _, antenna_full, twice = weights.shape
    frames = tm * groups * 8
    beams = twice // 2
    return pl.pallas_call(
        functools.partial(beam_kernel, wide, tm, first),
        grid=(channels,),
        in_specs=[
            pl.BlockSpec((devices, 128), lambda c: (0, 0)),
            pl.BlockSpec((devices, 1, groups, 16, antennas), lambda c: (0, c, 0, 0, 0)),
            pl.BlockSpec(memory_space=pl.ANY)
            if quarters
            else pl.BlockSpec((1, antenna_full, twice), lambda c: (c + first, 0, 0)),
        ],
        out_specs=[
            pl.BlockSpec((1, frames, beams), lambda c: (c, 0, 0)),
            pl.BlockSpec((devices, 128), lambda c: (0, 0)),
        ],
        out_shape=[
            jax.ShapeDtypeStruct((channels, frames, beams), jnp.float32),
            jax.ShapeDtypeStruct((devices, 128), jnp.float32),
        ],
        scratch_shapes=[
            pltpu.VMEM((2 * frames, antenna_full), jnp.bfloat16),
            pltpu.VMEM((1, 128), jnp.float32),
        ]
        + (
            [
                pltpu.VMEM((antenna_full, twice), jnp.bfloat16),
                pltpu.SemaphoreType.DMA((quarters,)),
            ]
            if quarters
            else []
        ),
        compiler_params=pltpu.CompilerParams(vmem_limit_bytes=48 * MIB),
        cost_estimate=pl.CostEstimate(
            flops=4 * channels * frames * antenna_full * twice,
            bytes_accessed=2 * channels * antenna_full * twice,
            transcendentals=0,
        ),
        name="beams",
    )(before, received, weights)


def level_kernel(wide, tm, mask_ref, count_ref, sums_ref, *refs):
    power_refs, out_ref = refs[:-1], refs[-1]
    channels = mask_ref.shape[0]
    _, frames, beams = power_refs[0].shape
    slots = [(ref, c) for ref in power_refs for c in range(ref.shape[0])]
    own_beams = beams // wide
    own_frames = frames // tm
    per_row = max(1, 128 // own_beams)
    sums = sums_ref[...]
    means = []
    for c in range(channels):
        means.append(jnp.sum(jnp.sum(mask_ref[c] * sums, axis=0, keepdims=True), axis=1, keepdims=True))
    mean = jnp.concatenate(means, axis=0) / count_ref[...]

    def level(f):
        value = jnp.concatenate([ref[c, f : f + 1, :] for ref, c in slots], axis=0)
        return (value / mean).astype(jnp.bfloat16)

    for start in range(0, frames, per_row):
        values = [level(f) for f in range(start, start + per_row)]
        for w in range(wide):
            piece = jnp.concatenate(
                [v[:, w * own_beams : (w + 1) * own_beams] for v in values], axis=1
            )
            m, at = divmod(start, own_frames)
            at *= own_beams
            out_ref[w * tm + m, :, at : at + per_row * own_beams] = piece


def form_levels(mask, count, sums, powers, wide, tm):
    channels = mask.shape[0]
    _, frames, beams = powers[0].shape
    lanes = frames // tm * (beams // wide)
    return pl.pallas_call(
        functools.partial(level_kernel, wide, tm),
        out_shape=jax.ShapeDtypeStruct((wide * tm, channels, lanes), jnp.bfloat16),
        compiler_params=pltpu.CompilerParams(vmem_limit_bytes=48 * MIB),
        name="levels",
    )(mask, count, sums, *powers)


def turn(source_ref, lane, lanes, target_ref, row):
    for start in range(0, lanes, 128):
        size = min(128, lanes - start)
        piece = source_ref[:, lane + start : lane + start + size].T
        target_ref[row + start : row + start + size, :] = piece


def dedisperse(turn_ref, pick_ref, sum_ref, row, frames, beams):
    chunk = 7
    for start in range(0, frames, chunk):
        stop = min(start + chunk, frames)
        held = jnp.concatenate(
            [
                turn_ref[(start + d) * beams : (stop + d) * beams, :]
                for d in range(MAXDELAY + 1)
            ],
            axis=1,
        )
        sum_ref[0, row + start * beams : row + stop * beams, :] = jnp.dot(
            held, pick_ref[...], preferred_element_type=jnp.float32
        )


def boxcars(channels, width_ref, sum_ref, stage_ref, out_ref, sems, row, beams):
    widths, rows, _ = stage_ref.shape
    for at in range(0, rows, 2 * beams):
        total = sum_ref[0, at : at + 2 * beams, :]
        for lag in range(1, WMAX):
            begin = at + lag * beams
            total = total + sum_ref[0, begin : begin + 2 * beams, :]
            sum_ref[lag, at : at + 2 * beams, :] = total
    copies = []
    for i in range(widths):
        expected = width_ref[i].astype(jnp.float32) * np.float32(channels)
        root = jnp.sqrt(jnp.full((1, stage_ref.shape[2]), expected, jnp.float32))
        stage_ref[i] = (sum_ref[width_ref[i] - 1, :rows, :] - expected) / root
        copy = pltpu.make_async_copy(
            stage_ref.at[i], out_ref.at[i, pl.ds(row, rows)], sems.at[i]
        )
        copy.start()
        copies.append(copy)
    for copy in copies:
        copy.wait()


def search_early_kernel(
    beams, width_ref, pick_ref, level_ref, out_ref, kept_ref, last_ref, turn_ref, sum_ref, stage_ref,
    sems,
):
    channels, lanes = level_ref.shape
    turn(level_ref, 0, lanes, turn_ref, 0)
    known = sum_ref.shape[1]
    dedisperse(turn_ref, pick_ref, sum_ref, 0, known // beams, beams)
    kept_ref[...] = sum_ref[0, known - kept_ref.shape[0] :, :]
    last_ref[...] = turn_ref[lanes - last_ref.shape[0] :, :]
    boxcars(channels, width_ref, sum_ref, stage_ref, out_ref, sems, 0, beams)


def search_late_kernel(
    beams, width_ref, pick_ref, last_ref, halo_ref, kept_ref, given_ref, out_ref, turn_ref,
    sum_ref, stage_ref, sems,
):
    held, channels = last_ref.shape
    turn_ref[:held, :] = last_ref[...]
    turn(halo_ref, 0, halo_ref.shape[1], turn_ref, held)
    kept = kept_ref.shape[0]
    sum_ref[0, :kept, :] = kept_ref[...]
    dedisperse(turn_ref, pick_ref, sum_ref, kept, sum_ref.shape[1] // beams - WMAX + 1, beams)
    row = out_ref.shape[1] - stage_ref.shape[1]
    boxcars(channels, width_ref, sum_ref, stage_ref, out_ref, sems, row, beams)


def search(box_widths, picks, levels, beams):
    trials = picks.shape[1]
    channels, lanes = levels.shape
    widths = box_widths.shape[0]
    lags = WMAX - 1
    frames = lanes // beams
    known = frames - MAXDELAY
    early = known - lags
    late = frames - early
    whole = pl.BlockSpec(memory_space=pltpu.VMEM)
    params = pltpu.CompilerParams(vmem_limit_bytes=32 * MIB)
    found, kept, last = pl.pallas_call(
        functools.partial(search_early_kernel, beams),
        in_specs=[pl.BlockSpec(memory_space=pltpu.SMEM), whole, whole],
        out_specs=[pl.BlockSpec(memory_space=pl.ANY), whole, whole],
        out_shape=[
            jax.ShapeDtypeStruct((widths, lanes, trials), jnp.float32),
            jax.ShapeDtypeStruct((lags * beams, trials), jnp.float32),
            jax.ShapeDtypeStruct((MAXDELAY * beams, channels), jnp.bfloat16),
        ],
        scratch_shapes=[
            pltpu.VMEM((lanes, channels), jnp.bfloat16),
            pltpu.VMEM((WMAX, known * beams, trials), jnp.float32),
            pltpu.VMEM((widths, early * beams, trials), jnp.float32),
            pltpu.SemaphoreType.DMA((widths,)),
        ],
        compiler_params=params,
        name="search_early",
    )(box_widths, picks, levels)
    blocks = lax.axis_size("tm")
    halo = lax.ppermute(
        levels[:, : (MAXDELAY + lags) * beams], "tm", [(i, (i - 1) % blocks) for i in range(blocks)]
    )
    return pl.pallas_call(
        functools.partial(search_late_kernel, beams),
        in_specs=[
            pl.BlockSpec(memory_space=pltpu.SMEM),
            whole,
            whole,
            whole,
            whole,
            pl.BlockSpec(memory_space=pl.ANY),
        ],
        out_specs=pl.BlockSpec(memory_space=pl.ANY),
        out_shape=jax.ShapeDtypeStruct((widths, lanes, trials), jnp.float32),
        scratch_shapes=[
            pltpu.VMEM(((MAXDELAY + MAXDELAY + lags) * beams, channels), jnp.bfloat16),
            pltpu.VMEM((WMAX, (late + lags) * beams, trials), jnp.float32),
            pltpu.VMEM((widths, late * beams, trials), jnp.float32),
            pltpu.SemaphoreType.DMA((widths,)),
        ],
        input_output_aliases={5: 0},
        compiler_params=params,
        name="search_late",
    )(box_widths, picks, last, halo, kept, found)


def exchange(value):
    return lax.all_to_all(value, AXES, split_axis=0, concat_axis=0, tiled=True)


def body(voltages, fir_taps, steering, band_widths, delays, box_widths):
    wide = lax.axis_size("wide")
    tm = lax.axis_size("tm")
    devices = wide * tm
    taps, channel_rows = fir_taps.shape
    antenna_local = voltages.shape[1]
    beam_count = steering.shape[0]
    sample_count = voltages.shape[2]
    frame_rows = sample_count // channel_rows
    total_frames = frame_rows * tm
    slots = channel_rows // devices
    own = lax.axis_index("wide") * tm + lax.axis_index("tm")
    own_ids = own * slots + jnp.arange(slots, dtype=jnp.int32)

    lookback = (taps - 1) * channel_rows
    halo = lax.ppermute(
        voltages[:, :, sample_count - lookback :], "tm", [(i, (i + 1) % tm) for i in range(tm)]
    )
    parts = slot_parts(slots)
    counts = [devices * part for part in parts]
    table = pltpu.with_memory_space_constraint(
        jnp.asarray(dft_rows(channel_rows, slots)), pltpu.HBM
    )
    fir_taps = pltpu.with_memory_space_constraint(fir_taps, pltpu.HBM)
    voltages = pltpu.with_memory_space_constraint(voltages, pltpu.HBM)
    early, tail = spectra(counts, table, halo, voltages, fir_taps)
    groups = frame_rows // 8

    def arrive(piece, part):
        received = exchange(piece.reshape(devices, part * groups * 16, antenna_local))
        return received.reshape(devices, part, groups, 16, antenna_local)

    frequency = 1.0 + own_ids.astype(jnp.float32) / channel_rows
    early, frequency, steering = lax.optimization_barrier((early, frequency, steering))
    weights = beam_weights(frequency, steering.T)
    early = arrive(early, parts[0])
    early, tail, weights = lax.optimization_barrier((early, tail, weights))
    sums = jnp.zeros((devices, 128), jnp.float32)
    power, sums = form_beams(early, weights, sums, 0, wide, tm, 0)
    late, sums = form_beams(
        arrive(tail, parts[1]), weights, sums, parts[0], wide, tm, 4
    )
    powers = [power, late]

    starts = jnp.cumsum(band_widths) - band_widths
    ids = jnp.arange(channel_rows, dtype=jnp.int32)
    bands = jnp.sum((ids[:, None] >= starts[None, :]).astype(jnp.int32), axis=1) - 1
    own_band = jnp.sum((own_ids[:, None] >= starts[None, :]).astype(jnp.int32), axis=1) - 1
    mask = (own_band[:, None] == bands[None, :]).astype(jnp.float32)
    mask = jnp.pad(mask.reshape(slots, devices, slots), ((0, 0), (0, 0), (0, 128 - slots)))
    count = jnp.sum(
        jnp.where(
            own_band[:, None] == jnp.arange(band_widths.shape[0], dtype=jnp.int32)[None, :],
            band_widths.astype(jnp.float32)[None, :] * (total_frames * beam_count),
            0.0,
        ),
        axis=1,
        keepdims=True,
    )
    levels = form_levels(mask, count, exchange(sums), powers, wide, tm)
    arrived = exchange(levels).reshape(channel_rows, levels.shape[2])

    steps = jnp.arange(MAXDELAY + 1, dtype=jnp.int32)
    picks = (delays.T[None, :, :] == steps[:, None, None]).astype(jnp.bfloat16)
    picks = picks.reshape((MAXDELAY + 1) * channel_rows, delays.shape[0])
    own_beams = beam_count // wide
    found = search(box_widths, picks, arrived, own_beams)
    found = found.reshape(box_widths.shape[0], frame_rows, own_beams, delays.shape[0])
    return found.transpose(3, 0, 1, 2)


def solution(mesh):
    return jax.shard_map(
        body,
        mesh=mesh,
        in_specs=(P(None, "wide", "tm"), P(), P(), P(), P(), P()),
        out_specs=P(None, None, "tm", "wide"),
        check_vma=False,
    )
```

```python
import functools
import math

import jax
import jax.numpy as jnp
import numpy as np
from jax import lax
from jax.experimental import pallas as pl
from jax.experimental.pallas import tpu as pltpu
from jax.sharding import PartitionSpec as P

MAXDELAY = 7
WMAX = 8
AXES = ("wide", "tm")
MIB = 1 << 20


def slot_parts(slots):
    late = max(1, slots // 8)
    return slots - late, late


def dft_rows(channel_rows, slots):
    positions = np.arange(channel_rows, dtype=np.int64)
    product = (positions[:, None] * positions[None, :] % channel_rows).astype(np.float32)
    angles = np.float32(2.0 * math.pi / channel_rows) * product
    cosine = np.cos(angles.astype(np.float64)).astype(np.float32)
    sines = np.sin(angles.astype(np.float64)).astype(np.float32)
    real_rows = np.concatenate([cosine.T, sines.T], axis=1)
    imag_rows = np.concatenate([-sines.T, cosine.T], axis=1)
    rows = np.stack([real_rows, imag_rows], axis=1).reshape(-1, slots, 2, 2 * channel_rows)
    first = 0
    ordered = []
    for count in slot_parts(slots):
        ordered.append(rows[:, first : first + count].reshape(-1, 2 * channel_rows))
        first += count
    return np.concatenate(ordered).astype(jnp.bfloat16)


def transform(inners, skip, taps_ref, table_ref, past_ref, volt_ref, part_ref):
    taps = taps_ref.shape[0]
    width = taps_ref.shape[1]
    for inner in inners:
        pieces = []
        for part in range(2):
            total = None
            for back in range(taps):
                if inner >= back:
                    at = (inner - back) * width
                    value = volt_ref[part, :, at : at + width]
                else:
                    at = skip + (taps - 1 + inner - back) * width
                    value = past_ref[part, :, at : at + width]
                term = taps_ref[back : back + 1, :] * value.astype(jnp.float32)
                total = term if total is None else total + term
            pieces.append(total.astype(jnp.bfloat16))
        filtered = jnp.concatenate(pieces, axis=1)
        spectrum = lax.dot_general(
            table_ref[...], filtered, (((1,), (1,)), ((), ())), preferred_element_type=jnp.float32
        )
        rows, antennas = spectrum.shape
        lanes = part_ref.shape[0] * 128
        if lanes > antennas:
            spectrum = jnp.concatenate(
                [spectrum, jnp.zeros((rows, lanes - antennas), jnp.float32)], axis=1
            )
        for half in range(lanes // 128):
            part_ref[half, pl.ds(inner, rows, stride=8), :] = spectrum[
                :, half * 128 : half * 128 + 128
            ]


def write_out(part_ref, out_refs, kept_ref=None, fresh=8):
    antennas = out_refs[0].shape[3]
    for half in range(part_ref.shape[0]):
        size = min(128, antennas - half * 128)
        first = 0
        for out_ref in out_refs:
            count = out_ref.shape[0]
            value = part_ref[half, first * 16 : (first + count) * 16]
            if kept_ref is not None:
                kept = kept_ref[half, first * 16 : (first + count) * 16]
                frame = lax.broadcasted_iota(jnp.int32, value.shape, 0) % 8
                value = jnp.where(frame < fresh, value, kept)
            value = value.astype(jnp.bfloat16).reshape(count, 16, 128)
            out_ref[:, 0, :, half * 128 : half * 128 + size] = value[:, :, :size]
            first += count


def spectra_kernel(skip, taps_ref, table_ref, past_ref, volt_ref, *rest):
    out_refs, kept_ref, part_ref = rest[:-2], rest[-2], rest[-1]
    taps = taps_ref.shape[0]

    @pl.when(pl.program_id(0) == 0)
    def _():
        transform(range(taps - 1, 8), 0, taps_ref, table_ref, past_ref, volt_ref, kept_ref)

    @pl.when(pl.program_id(0) > 0)
    def _():
        transform(range(8), skip, taps_ref, table_ref, past_ref, volt_ref, part_ref)
        write_out(part_ref, out_refs)


def spectra_first_kernel(taps_ref, table_ref, past_ref, volt_ref, kept_ref, *rest):
    count = (len(rest) - 1) // 2
    out_refs, part_ref = rest[count:-1], rest[-1]
    fresh = taps_ref.shape[0] - 1
    transform(range(fresh), 0, taps_ref, table_ref, past_ref, volt_ref, part_ref)
    write_out(part_ref, out_refs, kept_ref.at[pl.ds(pl.program_id(0), 1)], fresh)


def spectra(counts, table, halo, voltages, fir_taps):
    taps, width = fir_taps.shape
    antennas = voltages.shape[1]
    groups = voltages.shape[2] // (8 * width)
    part = pltpu.VMEM((-(-antennas // 128), 2 * width * 8, 128), jnp.float32)
    shapes = [pltpu.HBM((count, groups, 16, antennas), jnp.bfloat16) for count in counts]

    size = 128 if antennas % 128 == 0 else antennas

    def blocks(place, size):
        return [pl.BlockSpec((count, 1, 16, size), place) for count in counts]

    def cost(frames):
        return pl.CostEstimate(
            flops=8 * frames * antennas * width * width,
            bytes_accessed=8 * frames * antennas * width,
            transcendentals=0,
        )

    common = [
        pl.BlockSpec(fir_taps.shape, lambda g: (0, 0)),
        pl.BlockSpec(table.shape, lambda g: (0, 0)),
    ]
    *outgoing, kept = pl.pallas_call(
        functools.partial(spectra_kernel, (5 - taps) * width),
        grid=(groups,),
        in_specs=common
        + [
            pl.BlockSpec((2, antennas, 4 * width), lambda g: (0, 0, jnp.maximum(2 * g - 1, 1))),
            pl.BlockSpec((2, antennas, 8 * width), lambda g: (0, 0, g)),
        ],
        out_specs=blocks(lambda g: (0, jnp.maximum(g, 1), 0, 0), antennas)
        + [pl.BlockSpec(memory_space=pltpu.VMEM)],
        out_shape=shapes + [part],
        scratch_shapes=[part],
        compiler_params=pltpu.CompilerParams(vmem_limit_bytes=40 * MIB),
        cost_estimate=cost(8 * groups),
        name="spectra",
    )(fir_taps, table, voltages, voltages)
    kept = pltpu.with_memory_space_constraint(kept, pltpu.VMEM)
    return pl.pallas_call(
        spectra_first_kernel,
        grid=(antennas // size,),
        in_specs=common
        + [
            pl.BlockSpec((2, size, halo.shape[2]), lambda h: (0, h, 0)),
            pl.BlockSpec((2, size, 4 * width), lambda h: (0, h, 0)),
            pl.BlockSpec(memory_space=pltpu.VMEM),
        ]
        + [pl.BlockSpec(memory_space=pl.ANY)] * len(counts),
        out_specs=blocks(lambda h: (0, 0, 0, h), size),
        out_shape=shapes,
        scratch_shapes=[pltpu.VMEM((1, 2 * width * 8, 128), jnp.float32)],
        input_output_aliases={5 + i: i for i in range(len(counts))},
        compiler_params=pltpu.CompilerParams(vmem_limit_bytes=32 * MIB),
        cost_estimate=cost(taps - 1),
        name="spectra_first",
    )(fir_taps, table, halo, voltages, kept, *outgoing)


def sincos(phase):
    turns = jnp.round(phase * np.float32(1.0 / (2.0 * math.pi)))
    high = np.float32(6.28125)
    middle = np.float32(np.round((2.0 * math.pi - 6.28125) * 2.0**26) / 2.0**26)
    low = np.float32(2.0 * math.pi - 6.28125 - float(middle))
    rest = phase - turns * high
    rest = rest - turns * middle
    rest = rest - turns * low
    square = rest * rest
    s = np.float32(SIN_COEF[-1])
    for value in SIN_COEF[-2::-1]:
        s = s * square + np.float32(value)
    s = s * rest
    c = np.float32(COS_COEF[-1])
    for value in COS_COEF[-2::-1]:
        c = c * square + np.float32(value)
    return np.float32(1.0) - s * s, s * c


def half_angle_coefficients():
    top = (math.pi + 0.01) ** 2
    nodes = (np.cos((np.arange(400) + 0.5) * math.pi / 400) + 1.0) * 0.5 * top
    root = np.sqrt(nodes)
    fits = []
    for values, order in (
        (math.sqrt(2.0) * np.sin(root / 2) / root, 5),
        (math.sqrt(2.0) * np.cos(root / 2), 6),
    ):
        fit = np.polynomial.chebyshev.Chebyshev.fit(nodes, values, order - 1, domain=[0.0, top])
        fits.append([float(v) for v in fit.convert(kind=np.polynomial.Polynomial).coef])
    return fits


SIN_COEF, COS_COEF = half_angle_coefficients()


def weights_kernel(freq_ref, steer_ref, out_ref):
    channel = pl.program_id(1)
    beams = steer_ref.shape[1]
    frequency = freq_ref[channel]
    rows = steer_ref.shape[0]

    def step(index, carry):
        at = pl.ds(pl.multiple_of(index * 16, 16), 16)
        phase = np.float32(2.0 * math.pi) * (frequency * steer_ref[at, :])
        cosine, sines = sincos(phase)
        out_ref[0, at, :beams] = cosine.astype(jnp.bfloat16)
        out_ref[0, at, beams:] = sines.astype(jnp.bfloat16)
        return carry

    lax.fori_loop(0, rows // 16, step, 0)


def beam_weights(frequency, steering_t):
    antennas, beams = steering_t.shape
    channels = frequency.shape[0]
    block = min(512, antennas)
    return pl.pallas_call(
        weights_kernel,
        grid=(antennas // block, channels),
        in_specs=[
            pl.BlockSpec(memory_space=pltpu.SMEM),
            pl.BlockSpec((block, beams), lambda a, c: (a, 0)),
        ],
        out_specs=pl.BlockSpec((1, block, 2 * beams), lambda a, c: (c, a, 0)),
        out_shape=jax.ShapeDtypeStruct((channels, antennas, 2 * beams), jnp.bfloat16),
        compiler_params=pltpu.CompilerParams(vmem_limit_bytes=32 * MIB),
        cost_estimate=pl.CostEstimate(
            flops=30 * channels * antennas * beams,
            bytes_accessed=4 * channels * antennas * beams,
            transcendentals=2 * channels * antennas * beams,
        ),
        name="weights",
    )(frequency, steering_t)


def beam_kernel(
    wide, tm, first, before_ref, data_ref, weight_ref, power_ref, sum_ref, gather_ref, acc_ref,
    *rest,
):
    channel = pl.program_id(0)
    copies = []
    if rest:
        held_ref, sems = rest
        steps = sems.shape[0]
        depth = held_ref.shape[0] // steps
        for step in range(steps):
            rows = pl.ds(step * depth, depth)
            copies.append(
                pltpu.make_async_copy(
                    weight_ref.at[channel + first, rows], held_ref.at[rows], sems.at[step]
                )
            )
            copies[-1].start()
    groups = data_ref.shape[2]
    antennas = data_ref.shape[4]
    rows = groups * 16
    for w in range(wide):
        for m in range(tm):
            gather_ref[m * rows : (m + 1) * rows, w * antennas : (w + 1) * antennas] = data_ref[
                w * tm + m, 0
            ].reshape(rows, antennas)
    if copies:
        products = None
        for step, copy in enumerate(copies):
            copy.wait()
            own = slice(step * depth, (step + 1) * depth)
            term = jnp.dot(
                gather_ref[:, own], held_ref[own, :], preferred_element_type=jnp.float32
            )
            products = term if products is None else products + term
    else:
        products = jnp.dot(gather_ref[...], weight_ref[0], preferred_element_type=jnp.float32)
    beams = products.shape[1] // 2
    products = products.reshape(tm * groups, 2, 8, 2 * beams)
    real_in = products[:, 0]
    imag_in = products[:, 1]
    beam_real = real_in[..., :beams] + imag_in[..., beams:]
    beam_imag = imag_in[..., :beams] - real_in[..., beams:]
    power = beam_real * beam_real + beam_imag * beam_imag
    power_ref[0] = power.reshape(tm * groups * 8, beams)
    total = jnp.sum(jnp.sum(power, axis=0), axis=(0, 1), keepdims=True)
    lane = lax.broadcasted_iota(jnp.int32, acc_ref.shape, 1)

    @pl.when(channel == 0)
    def _():
        acc_ref[...] = before_ref[:1, :]

    acc_ref[...] = jnp.where(lane == channel + first, total, acc_ref[...])

    @pl.when(channel == pl.num_programs(0) - 1)
    def _():
        sum_ref[...] = jnp.broadcast_to(acc_ref[...], sum_ref.shape)


def form_beams(received, weights, before, first, wide, tm, quarters):
    devices, channels, groups, _, antennas = received.shape
    _, antenna_full, twice = weights.shape
    frames = tm * groups * 8
    beams = twice // 2
    return pl.pallas_call(
        functools.partial(beam_kernel, wide, tm, first),
        grid=(channels,),
        in_specs=[
            pl.BlockSpec((devices, 128), lambda c: (0, 0)),
            pl.BlockSpec((devices, 1, groups, 16, antennas), lambda c: (0, c, 0, 0, 0)),
            pl.BlockSpec(memory_space=pl.ANY)
            if quarters
            else pl.BlockSpec((1, antenna_full, twice), lambda c: (c + first, 0, 0)),
        ],
        out_specs=[
            pl.BlockSpec((1, frames, beams), lambda c: (c, 0, 0)),
            pl.BlockSpec((devices, 128), lambda c: (0, 0)),
        ],
        out_shape=[
            jax.ShapeDtypeStruct((channels, frames, beams), jnp.float32),
            jax.ShapeDtypeStruct((devices, 128), jnp.float32),
        ],
        scratch_shapes=[
            pltpu.VMEM((2 * frames, antenna_full), jnp.bfloat16),
            pltpu.VMEM((1, 128), jnp.float32),
        ]
        + (
            [
                pltpu.VMEM((antenna_full, twice), jnp.bfloat16),
                pltpu.SemaphoreType.DMA((quarters,)),
            ]
            if quarters
            else []
        ),
        compiler_params=pltpu.CompilerParams(vmem_limit_bytes=48 * MIB),
        cost_estimate=pl.CostEstimate(
            flops=4 * channels * frames * antenna_full * twice,
            bytes_accessed=2 * channels * antenna_full * twice,
            transcendentals=0,
        ),
        name="beams",
    )(before, received, weights)


def level_kernel(wide, tm, mask_ref, count_ref, sums_ref, *refs):
    power_refs, out_ref = refs[:-1], refs[-1]
    channels = mask_ref.shape[0]
    _, frames, beams = power_refs[0].shape
    slots = [(ref, c) for ref in power_refs for c in range(ref.shape[0])]
    own_beams = beams // wide
    own_frames = frames // tm
    per_row = max(1, 128 // own_beams)
    sums = sums_ref[...]
    means = []
    for c in range(channels):
        means.append(jnp.sum(jnp.sum(mask_ref[c] * sums, axis=0, keepdims=True), axis=1, keepdims=True))
    mean = jnp.concatenate(means, axis=0) / count_ref[...]

    def level(f):
        value = jnp.concatenate([ref[c, f : f + 1, :] for ref, c in slots], axis=0)
        return (value / mean).astype(jnp.bfloat16)

    for start in range(0, frames, per_row):
        values = [level(f) for f in range(start, start + per_row)]
        for w in range(wide):
            piece = jnp.concatenate(
                [v[:, w * own_beams : (w + 1) * own_beams] for v in values], axis=1
            )
            m, at = divmod(start, own_frames)
            at *= own_beams
            out_ref[w * tm + m, :, at : at + per_row * own_beams] = piece


def form_levels(mask, count, sums, powers, wide, tm):
    channels = mask.shape[0]
    _, frames, beams = powers[0].shape
    lanes = frames // tm * (beams // wide)
    return pl.pallas_call(
        functools.partial(level_kernel, wide, tm),
        out_shape=jax.ShapeDtypeStruct((wide * tm, channels, lanes), jnp.bfloat16),
        compiler_params=pltpu.CompilerParams(vmem_limit_bytes=48 * MIB),
        name="levels",
    )(mask, count, sums, *powers)


def turn(source_ref, lane, lanes, target_ref, row):
    for start in range(0, lanes, 128):
        size = min(128, lanes - start)
        piece = source_ref[:, lane + start : lane + start + size].T
        target_ref[row + start : row + start + size, :] = piece


def dedisperse(turn_ref, pick_ref, sum_ref, row, frames, beams):
    chunk = 7
    for start in range(0, frames, chunk):
        stop = min(start + chunk, frames)
        held = jnp.concatenate(
            [
                turn_ref[(start + d) * beams : (stop + d) * beams, :]
                for d in range(MAXDELAY + 1)
            ],
            axis=1,
        )
        sum_ref[0, row + start * beams : row + stop * beams, :] = jnp.dot(
            held, pick_ref[...], preferred_element_type=jnp.float32
        )


def boxcars(channels, width_ref, sum_ref, stage_ref, out_ref, sems, row, beams):
    widths, rows, _ = stage_ref.shape
    for at in range(0, rows, 2 * beams):
        total = sum_ref[0, at : at + 2 * beams, :]
        for lag in range(1, WMAX):
            begin = at + lag * beams
            total = total + sum_ref[0, begin : begin + 2 * beams, :]
            sum_ref[lag, at : at + 2 * beams, :] = total
    copies = []
    for i in range(widths):
        expected = width_ref[i].astype(jnp.float32) * np.float32(channels)
        root = jnp.sqrt(jnp.full((1, stage_ref.shape[2]), expected, jnp.float32))
        stage_ref[i] = (sum_ref[width_ref[i] - 1, :rows, :] - expected) / root
        copy = pltpu.make_async_copy(
            stage_ref.at[i], out_ref.at[i, pl.ds(row, rows)], sems.at[i]
        )
        copy.start()
        copies.append(copy)
    for copy in copies:
        copy.wait()


def search_early_kernel(
    beams, width_ref, pick_ref, level_ref, out_ref, kept_ref, last_ref, turn_ref, sum_ref, stage_ref,
    sems,
):
    channels, lanes = level_ref.shape
    turn(level_ref, 0, lanes, turn_ref, 0)
    known = sum_ref.shape[1]
    dedisperse(turn_ref, pick_ref, sum_ref, 0, known // beams, beams)
    kept_ref[...] = sum_ref[0, known - kept_ref.shape[0] :, :]
    last_ref[...] = turn_ref[lanes - last_ref.shape[0] :, :]
    boxcars(channels, width_ref, sum_ref, stage_ref, out_ref, sems, 0, beams)


def search_late_kernel(
    beams, width_ref, pick_ref, last_ref, halo_ref, kept_ref, given_ref, out_ref, turn_ref,
    sum_ref, stage_ref, sems,
):
    held, channels = last_ref.shape
    turn_ref[:held, :] = last_ref[...]
    turn(halo_ref, 0, halo_ref.shape[1], turn_ref, held)
    kept = kept_ref.shape[0]
    sum_ref[0, :kept, :] = kept_ref[...]
    dedisperse(turn_ref, pick_ref, sum_ref, kept, sum_ref.shape[1] // beams - WMAX + 1, beams)
    row = out_ref.shape[1] - stage_ref.shape[1]
    boxcars(channels, width_ref, sum_ref, stage_ref, out_ref, sems, row, beams)


def search(box_widths, picks, levels, beams):
    trials = picks.shape[1]
    channels, lanes = levels.shape
    widths = box_widths.shape[0]
    lags = WMAX - 1
    frames = lanes // beams
    known = frames - MAXDELAY
    early = known - lags
    late = frames - early
    whole = pl.BlockSpec(memory_space=pltpu.VMEM)
    params = pltpu.CompilerParams(vmem_limit_bytes=32 * MIB)
    found, kept, last = pl.pallas_call(
        functools.partial(search_early_kernel, beams),
        in_specs=[pl.BlockSpec(memory_space=pltpu.SMEM), whole, whole],
        out_specs=[pl.BlockSpec(memory_space=pl.ANY), whole, whole],
        out_shape=[
            jax.ShapeDtypeStruct((widths, lanes, trials), jnp.float32),
            jax.ShapeDtypeStruct((lags * beams, trials), jnp.float32),
            jax.ShapeDtypeStruct((MAXDELAY * beams, channels), jnp.bfloat16),
        ],
        scratch_shapes=[
            pltpu.VMEM((lanes, channels), jnp.bfloat16),
            pltpu.VMEM((WMAX, known * beams, trials), jnp.float32),
            pltpu.VMEM((widths, early * beams, trials), jnp.float32),
            pltpu.SemaphoreType.DMA((widths,)),
        ],
        compiler_params=params,
        name="search_early",
    )(box_widths, picks, levels)
    blocks = lax.axis_size("tm")
    halo = lax.ppermute(
        levels[:, : (MAXDELAY + lags) * beams], "tm", [(i, (i - 1) % blocks) for i in range(blocks)]
    )
    return pl.pallas_call(
        functools.partial(search_late_kernel, beams),
        in_specs=[
            pl.BlockSpec(memory_space=pltpu.SMEM),
            whole,
            whole,
            whole,
            whole,
            pl.BlockSpec(memory_space=pl.ANY),
        ],
        out_specs=pl.BlockSpec(memory_space=pl.ANY),
        out_shape=jax.ShapeDtypeStruct((widths, lanes, trials), jnp.float32),
        scratch_shapes=[
            pltpu.VMEM(((MAXDELAY + MAXDELAY + lags) * beams, channels), jnp.bfloat16),
            pltpu.VMEM((WMAX, (late + lags) * beams, trials), jnp.float32),
            pltpu.VMEM((widths, late * beams, trials), jnp.float32),
            pltpu.SemaphoreType.DMA((widths,)),
        ],
        input_output_aliases={5: 0},
        compiler_params=params,
        name="search_late",
    )(box_widths, picks, last, halo, kept, found)


def exchange(value):
    return lax.all_to_all(value, AXES, split_axis=0, concat_axis=0, tiled=True)


def body(voltages, fir_taps, steering, band_widths, delays, box_widths):
    wide = lax.axis_size("wide")
    tm = lax.axis_size("tm")
    devices = wide * tm
    taps, channel_rows = fir_taps.shape
    antenna_local = voltages.shape[1]
    beam_count = steering.shape[0]
    sample_count = voltages.shape[2]
    frame_rows = sample_count // channel_rows
    total_frames = frame_rows * tm
    slots = channel_rows // devices
    own = lax.axis_index("wide") * tm + lax.axis_index("tm")
    own_ids = own * slots + jnp.arange(slots, dtype=jnp.int32)

    lookback = (taps - 1) * channel_rows
    halo = lax.ppermute(
        voltages[:, :, sample_count - lookback :], "tm", [(i, (i + 1) % tm) for i in range(tm)]
    )
    parts = slot_parts(slots)
    counts = [devices * part for part in parts]
    table = pltpu.with_memory_space_constraint(
        jnp.asarray(dft_rows(channel_rows, slots)), pltpu.HBM
    )
    fir_taps = pltpu.with_memory_space_constraint(fir_taps, pltpu.HBM)
    voltages = pltpu.with_memory_space_constraint(voltages, pltpu.HBM)
    early, tail = spectra(counts, table, halo, voltages, fir_taps)
    groups = frame_rows // 8

    def arrive(piece, part):
        received = exchange(piece.reshape(devices, part * groups * 16, antenna_local))
        return received.reshape(devices, part, groups, 16, antenna_local)

    frequency = 1.0 + own_ids.astype(jnp.float32) / channel_rows
    early, frequency, steering = lax.optimization_barrier((early, frequency, steering))
    weights = beam_weights(frequency, steering.T)
    early = arrive(early, parts[0])
    early, tail, weights = lax.optimization_barrier((early, tail, weights))
    sums = jnp.zeros((devices, 128), jnp.float32)
    power, sums = form_beams(early, weights, sums, 0, wide, tm, 0)
    late, sums = form_beams(
        arrive(tail, parts[1]), weights, sums, parts[0], wide, tm, 8
    )
    powers = [power, late]

    starts = jnp.cumsum(band_widths) - band_widths
    ids = jnp.arange(channel_rows, dtype=jnp.int32)
    bands = jnp.sum((ids[:, None] >= starts[None, :]).astype(jnp.int32), axis=1) - 1
    own_band = jnp.sum((own_ids[:, None] >= starts[None, :]).astype(jnp.int32), axis=1) - 1
    mask = (own_band[:, None] == bands[None, :]).astype(jnp.float32)
    mask = jnp.pad(mask.reshape(slots, devices, slots), ((0, 0), (0, 0), (0, 128 - slots)))
    count = jnp.sum(
        jnp.where(
            own_band[:, None] == jnp.arange(band_widths.shape[0], dtype=jnp.int32)[None, :],
            band_widths.astype(jnp.float32)[None, :] * (total_frames * beam_count),
            0.0,
        ),
        axis=1,
        keepdims=True,
    )
    levels = form_levels(mask, count, exchange(sums), powers, wide, tm)
    arrived = exchange(levels).reshape(channel_rows, levels.shape[2])

    steps = jnp.arange(MAXDELAY + 1, dtype=jnp.int32)
    picks = (delays.T[None, :, :] == steps[:, None, None]).astype(jnp.bfloat16)
    picks = picks.reshape((MAXDELAY + 1) * channel_rows, delays.shape[0])
    own_beams = beam_count // wide
    found = search(box_widths, picks, arrived, own_beams)
    found = found.reshape(box_widths.shape[0], frame_rows, own_beams, delays.shape[0])
    return found.transpose(3, 0, 1, 2)


def solution(mesh):
    return jax.shard_map(
        body,
        mesh=mesh,
        in_specs=(P(None, "wide", "tm"), P(), P(), P(), P(), P()),
        out_specs=P(None, None, "tm", "wide"),
        check_vma=False,
    )
```
